128 devices in a mesh: cache: 8 (over x, core), space: 8 (over z, y_hi), head: 2 (over y_lo).
Axes of the slice: x: 4, y: 4 (y_hi: 2, y_lo: 2; y = y_hi * 2 + y_lo), z: 4, core: 2. Of those that a mesh axis runs over, the one named last changes fastest.
Arguments:
- queries: bfloat16 [32, 640, 2560], P('cache', 'space', 'head'), may hold values from -8 to 8, as said below
- keys: bfloat16 [32, 640, 2560], P('cache', 'space', 'head'), may hold values from -8 to 8, as said below
- values: bfloat16 [32, 640, 2560], P('cache', 'space', 'head'), may hold values from -6 to 6
- cache_keys: bfloat16 [16, 640, 2560], P('cache', 'space', 'head'), may hold values from -8 to 8
- cache_values: bfloat16 [16, 640, 2560], P('cache', 'space', 'head'), may hold values from -6 to 6
- window: int32 [32, 2], replicated, may hold values from 0 to 15, as said below
- span_slot: int32 [16], replicated, may hold values from 0 to 15, as said below
- counts: int32 [16], replicated, may hold values from 320 to 640
- out_weight: bfloat16 [2560, 5120], P('head'), may hold values from -0.125 to 0.125
Outputs:
- mixed: bfloat16 [32, 640, 5120], P('cache', 'space', 'head')
The draws below stay inside these ranges and needn't reach their ends.
Inputs may be any that keep to these rules, and one draw needn't show every extreme that they name: `queries`: values of order one. `keys`: values of order one. `window`: for every block of 4 current spans (rows b * 4 .. (b + 1) * 4 - 1) and every cache group g, the block's entries name exactly one cached span id whose slot lies in g * 2 .. (g + 1) * 2 - 1; entries may repeat. `span_slot`: each slot once.
All inputs are finite; a program needn't handle non-finite values.
Results may differ from the reference program's by a relative error of at most 0.0052.
Values may be sent and summed in bfloat16 or wider, within the bound.
No kernel may reach another device: no remote copies, remote signals or barrier semaphores. Data moves between devices by JAX's collectives and lax.ppermute only.
A program may use at most 192 MiB of HBM per device.

```python
import math
import jax
import jax.numpy as jnp
from jax import lax

D = 5120
HEADS = 20
HD = 128
WIN = 2
CPG = 4
OWN = 2
CUR = 32
SLOTS = 16
SPAN = 640
FEAT = 2560


def slot_order(key):
    return jax.random.permutation(key, SLOTS).astype(jnp.int32)


def draw_span_slot(key, part):
    return slot_order(key)


def draw_window(key, part):
    order = slot_order(key)
    inverse = jnp.argsort(order).astype(jnp.int32)
    key = jax.random.fold_in(key, 5)
    groups = CUR // CPG
    picks = jax.random.randint(jax.random.fold_in(key, 1), (groups, groups), 0, OWN).astype(jnp.int32)
    owned = jnp.arange(groups, dtype=jnp.int32)[None, :] * OWN + picks
    extra = jax.random.randint(jax.random.fold_in(key, 2), (groups, CPG * WIN - groups), 0, groups).astype(jnp.int32)
    firsts = jnp.broadcast_to(jnp.arange(groups, dtype=jnp.int32)[None, :], (groups, groups))
    columns = jnp.concatenate([firsts, extra], 1)
    shuffle_keys = jax.random.split(jax.random.fold_in(key, 3), groups)
    columns = jax.vmap(lambda one_key, row: jax.random.permutation(one_key, row))(shuffle_keys, columns)
    chosen = jnp.take_along_axis(owned, columns, axis=1)
    return inverse[chosen].reshape(CUR, WIN).astype(jnp.int32)


def draw_queries(key, part):
    key = jax.random.fold_in(key, 7)
    base = jnp.clip(1.6 * jax.random.normal(key, (CUR, SPAN, FEAT), jnp.float32), -8.0, 8.0)
    return base.astype(jnp.bfloat16)


def draw_keys(key, part):
    key = jax.random.fold_in(key, 11)
    base = jnp.clip(1.6 * jax.random.normal(key, (CUR, SPAN, FEAT), jnp.float32), -8.0, 8.0)
    return base.astype(jnp.bfloat16)


def set_ends(result, key, smallest, largest):
    longest = result.shape.index(max(result.shape))
    spots = []
    for shift in (0, 1):
        where = [jax.random.randint(jax.random.fold_in(key, axis), (), 0, length) for axis, length in enumerate(result.shape)]
        where[longest] = (where[longest] + shift) % result.shape[longest]
        spots.append(tuple(where))
    return result.at[spots[0]].set(smallest).at[spots[1]].set(largest)


def steps_of(key, extent, cuts, smallest, largest):
    def one(position, parts):
        heights = jax.random.uniform(jax.random.fold_in(jax.random.fold_in(key, 6), position), (parts,), jnp.float32, smallest / len(cuts), largest / len(cuts))
        return jnp.repeat(jnp.exp(heights), extent[position] // parts).reshape((-1,) + (1,) * (len(extent) - position - 1))

    gain = one(*cuts[0])
    for cut in cuts[1:]:
        gain = gain * one(*cut)
    return gain


def scatter_about(rng, extent, scale, bound, cuts=(), kind=jnp.bfloat16):
    factor_of = steps_of(rng, extent, cuts, -0.22, 0.18) if cuts else 1.0
    entries = jax.random.normal(rng, extent, jnp.float32) * scale * factor_of
    return jnp.minimum(jnp.maximum(entries, -bound), bound).astype(kind)


def setup_inputs(seed: int = 0) -> dict:
    key_of = jax.random.split(jax.random.key(seed), 10)
    return {
        "queries": draw_queries(jax.random.fold_in(key_of[9], 71), 0),
        "keys": draw_keys(jax.random.fold_in(key_of[9], 71), 0),
        "values": scatter_about(key_of[2], (CUR, SPAN, FEAT), 1.0, 6.0, ((0, 8), (1, 8), (2, 2))),
        "cache_keys": scatter_about(key_of[3], (SLOTS, SPAN, FEAT), 1.6, 8.0, ((0, 8), (1, 8), (2, 2))),
        "cache_values": scatter_about(key_of[4], (SLOTS, SPAN, FEAT), 1.0, 6.0, ((0, 8), (1, 8), (2, 2))),
        "window": draw_window(jax.random.fold_in(key_of[9], 71), 0),
        "span_slot": draw_span_slot(jax.random.fold_in(key_of[9], 71), 0),
        "counts": set_ends(jax.random.randint(key_of[7], (SLOTS,), SPAN // 2, SPAN + 1), jax.random.fold_in(key_of[7], 1), SPAN // 2, SPAN).astype(jnp.int32),
        "out_weight": scatter_about(key_of[8], (FEAT, D), FEAT ** -0.5, 0.125, ((0, 2),)),
    }


def reference(queries, keys, values, cache_keys, cache_values, window, span_slot, counts, out_weight):
    scale = 1.0 / math.sqrt(HD)
    positions = jnp.arange(SPAN, dtype=jnp.int32)

    def one_span(current):
        chosen = window[current]
        slots = span_slot[chosen]
        key_set = jnp.concatenate([keys[current][None], cache_keys[slots]], 0).reshape((1 + WIN) * SPAN, HEADS, HD)
        value_set = jnp.concatenate([values[current][None], cache_values[slots]], 0).reshape((1 + WIN) * SPAN, HEADS, HD)
        own_valid = jnp.ones((1, SPAN), dtype=jnp.int32)
        cached_valid = (positions[None, :] < counts[chosen][:, None]).astype(jnp.int32)
        valid = jnp.concatenate([own_valid, cached_valid], 0).reshape(-1)
        query_set = queries[current].reshape(SPAN, HEADS, HD)

        def one_head(pieces):
            query_head, key_head, value_head = pieces
            scores = jnp.dot(query_head, key_head.T, preferred_element_type=jnp.float32) * scale
            scores = jnp.where(valid[None, :] > 0, scores, -jnp.inf)
            top = lax.optimization_barrier(jnp.max(scores, axis=1, keepdims=True))
            weights = jnp.exp(scores - top)
            totals = lax.optimization_barrier(jnp.sum(weights, axis=1, keepdims=True))
            numer = jnp.dot(weights.astype(jnp.bfloat16), value_head, preferred_element_type=jnp.float32)
            return (numer / totals).astype(jnp.bfloat16)
        attended = lax.map(one_head, (jnp.transpose(query_set, (1, 0, 2)), jnp.transpose(key_set, (1, 0, 2)), jnp.transpose(value_set, (1, 0, 2))))
        attended = jnp.transpose(attended, (1, 0, 2)).reshape(SPAN, FEAT)
        return jnp.dot(attended, out_weight, preferred_element_type=jnp.float32).astype(jnp.bfloat16)
    return lax.map(one_span, jnp.arange(CUR, dtype=jnp.int32))
```

```python
import math

import jax
import jax.numpy as jnp
from jax import lax
from jax.experimental import pallas as pl
from jax.experimental.pallas import tpu as pltpu
from jax.sharding import PartitionSpec as P

HD = 128
WIN = 2
SPANS = 4
GROUPS = 8
SPACE = 8
ROWS = 80
SPAN = SPACE * ROWS
HEADS = 10
WIDE = SPACE * HD
PAIRS = 5
UNITS = 3 * PAIRS + 2 * WIN
VMEM = pl.BlockSpec(memory_space=pltpu.VMEM)
SMEM = pl.BlockSpec(memory_space=pltpu.SMEM)
MIB = 1 << 20


def params(mib):
    return pltpu.CompilerParams(vmem_limit_bytes=mib * MIB)


def picked(window, span_slot, block, group):
    place = jnp.int32(0)
    for span in range(SPANS):
        for w in range(WIN):
            slot = span_slot[window[block * SPANS + span, w]]
            place = jnp.where((slot >> 1) == group, slot & 1, place)
    return place


def pack_slots(window, span_slot, cache_keys, cache_values, by_head, *rest):
    me = lax.axis_index("cache")
    for head in range(SPACE):
        for kv, source in enumerate((cache_keys, cache_values)):
            for slot in range(2):
                row = (kv * 2 + slot) * ROWS
                by_head[head, row : row + ROWS] = source[slot, :, head * HD : (head + 1) * HD]
    for step in range(GROUPS):
        slot = picked(window, span_slot, (me + step) & 7, me)
        for kv, source in enumerate((cache_keys, cache_values)):
            rest[step][kv] = source[slot, :, WIDE:]


def pack_wide(window, span_slot, by_head, sent):
    me = lax.axis_index("cache")
    for block in range(GROUPS):
        slot = picked(window, span_slot, block, me)
        for kv in range(2):
            for space in range(SPACE):
                row = (kv * SPACE + space) * ROWS
                start = pl.multiple_of((kv * 2 + slot) * ROWS, 16)
                sent[block, row : row + ROWS] = by_head[space, pl.ds(start, ROWS)]


def pack_pairs(window, span_slot, queries, keys, values, *refs):
    rest, sent, held = refs[:GROUPS], refs[GROUPS : GROUPS + SPACE], refs[-1]
    group = lax.axis_index("cache")
    me = lax.axis_index("space")
    for step in range(GROUPS):
        held[(group - step) & 7] = rest[step][...]
    for step in range(SPACE):
        to = (me + step) & 7
        span = to >> 1
        wide = pl.ds(pl.multiple_of(to * HD, HD), HD)
        last = pl.multiple_of((to & 1) * HD, HD)
        for kind, source in enumerate((queries, keys, values)):
            for pair in range(SPANS):
                sent[step][kind * PAIRS + pair] = source[pair, :, wide]
            sent[step][kind * PAIRS + SPANS] = source[
                span, :, pl.ds(pl.multiple_of(WIDE + last, HD), HD)
            ]
        for w in range(WIN):
            owner = span_slot[window[group * SPANS + span, w]] >> 1
            for kv in range(2):
                sent[step][3 * PAIRS + 2 * w + kv] = held[owner, kv, :, pl.ds(last, HD)]


def attend(window, span_slot, counts, *refs):
    came, wide, out, q_all, k_all, v_all, done = (refs[:SPACE],) + refs[SPACE:]
    group = lax.axis_index("cache")
    me = lax.axis_index("space")
    factor = math.log2(math.e) / math.sqrt(HD)
    spots = lax.broadcasted_iota(jnp.int32, (SPAN, HD), 0)
    v_all[0:SPAN, HD:] = jnp.ones((SPAN, HD), jnp.bfloat16)

    @pl.loop(0, PAIRS)
    def _(pair):
        for step in range(SPACE):
            rows = pl.ds(step * ROWS, ROWS)
            q_all[rows] = came[step][pair]
            k_all[rows] = came[step][PAIRS + pair]
            v_all[rows, 0:HD] = came[step][2 * PAIRS + pair]
        span = jnp.where(pair < SPANS, pair, me >> 1)
        for w in range(WIN):
            chosen = window[group * SPANS + span, w]
            limit = counts[chosen]
            owner = span_slot[chosen] >> 1
            base = (1 + w) * SPAN
            part = pl.ds(base, SPAN)

            @pl.when(pair < SPANS)
            def _():
                k_all[part] = wide[owner, 0:SPAN]
                v_all[part, 0:HD] = wide[owner, SPAN:]

            @pl.when(pair == SPANS)
            def _():
                for step in range(SPACE):
                    start = pl.multiple_of(base + ((me - step) & 7) * ROWS, 16)
                    k_all[pl.ds(start, ROWS)] = came[step][3 * PAIRS + 2 * w]
                    v_all[pl.ds(start, ROWS), 0:HD] = came[step][3 * PAIRS + 2 * w + 1]

            valid = spots < limit
            first = jnp.broadcast_to(k_all[base : base + 1].astype(jnp.float32), (SPAN, HD))
            k_all[part] = jnp.where(valid, k_all[part].astype(jnp.float32), first).astype(
                jnp.bfloat16
            )
            v_all[part, 0:HD] = jnp.where(
                valid, v_all[part, 0:HD].astype(jnp.float32), 0.0
            ).astype(jnp.bfloat16)
            v_all[part, HD:] = jnp.where(valid, 1.0, 0.0).astype(jnp.bfloat16)
        block = SPAN // 2
        for start in range(0, SPAN, block):
            scores = lax.dot_general(
                q_all[start : start + block],
                k_all[...],
                (((1,), (1,)), ((), ())),
                preferred_element_type=jnp.float32,
            )
            top = jnp.max(scores, axis=1, keepdims=True)
            weights = jnp.exp2((scores - top) * factor).astype(jnp.bfloat16)
            both = jnp.dot(weights, v_all[...], preferred_element_type=jnp.float32)
            done[start : start + block] = (both[:, 0:HD] / both[:, HD:]).astype(jnp.bfloat16)
        for step in range(SPACE):
            to = (me - step) & 7
            for half in range(2):
                out[2 * to + half, pair] = done[step * ROWS : (step + 1) * ROWS]


def project(half, came, own_weight, other_weight, out, features):
    @pl.when(pl.program_id(0) == 0)
    def _():
        for part in range(2):
            source = half[0] if part == 0 else 1 - half[0]
            for space in range(SPACE):
                for pair in range(SPANS):
                    features[part, pair * ROWS : (pair + 1) * ROWS, space * HD : (space + 1) * HD] = (
                        came[2 * space + source, pair * ROWS : (pair + 1) * ROWS]
                    )
                span, column = space // 2, WIDE + space % 2 * HD
                features[part, span * ROWS : (span + 1) * ROWS, column : column + HD] = came[
                    2 * space + source, SPANS * ROWS :
                ]

    total = jnp.dot(features[0], own_weight[...], preferred_element_type=jnp.float32)
    total += jnp.dot(features[1], other_weight[...], preferred_element_type=jnp.float32)
    out[...] = total.astype(jnp.bfloat16)


def shift(x, axis, step):
    return lax.ppermute(x, axis, [(i, (i + step) % 8) for i in range(8)])


def on_device(
    queries, keys, values, cache_keys, cache_values, window, span_slot, counts, out_weight
):
    bf16 = jnp.bfloat16
    shape = jax.ShapeDtypeStruct
    group = lax.axis_index("cache")
    half = lax.axis_index("head")
    depth, width = out_weight.shape
    columns = width // 2

    rows = depth // GROUPS
    lent = lax.dynamic_slice(out_weight, (group * rows, (1 - half) * columns), (rows, columns))
    lent = lax.ppermute(lent, "head", [(0, 1), (1, 0)])
    other_weight = lax.all_gather(lent, "cache", axis=0, tiled=True)

    by_head, *rest = pl.pallas_call(
        pack_slots,
        out_shape=[shape((SPACE, 4 * ROWS, HD), bf16)]
        + [shape((2, ROWS, 2 * HD), bf16)] * GROUPS,
        in_specs=[SMEM] * 2 + [VMEM] * 2,
        out_specs=[VMEM] * (1 + GROUPS),
        compiler_params=params(16),
        name="pack_slots",
    )(window, span_slot, cache_keys, cache_values)
    by_head = lax.all_to_all(by_head, "space", split_axis=0, concat_axis=0, tiled=True)
    rest = [rest[0]] + [shift(rest[step], "cache", step) for step in range(1, GROUPS)]

    wide = pl.pallas_call(
        pack_wide,
        out_shape=shape((GROUPS, 2 * SPAN, HD), bf16),
        in_specs=[SMEM] * 2 + [VMEM],
        out_specs=VMEM,
        compiler_params=params(16),
        name="pack_wide",
    )(window, span_slot, by_head)
    wide = lax.all_to_all(wide, "cache", split_axis=0, concat_axis=0, tiled=True)

    pairs = pl.pallas_call(
        pack_pairs,
        out_shape=[shape((UNITS, ROWS, HD), bf16)] * SPACE,
        in_specs=[SMEM] * 2 + [VMEM] * (3 + GROUPS),
        out_specs=[VMEM] * SPACE,
        scratch_shapes=[pltpu.VMEM((GROUPS, 2, ROWS, 2 * HD), bf16)],
        compiler_params=params(16),
        name="pack_pairs",
    )(window, span_slot, queries, keys, values, *rest)
    came = [pairs[0]] + [shift(pairs[step], "space", step) for step in range(1, SPACE)]

    attended = pl.pallas_call(
        attend,
        out_shape=shape((2 * SPACE, PAIRS, ROWS, HD), bf16),
        in_specs=[SMEM] * 3 + [VMEM] * (SPACE + 1),
        out_specs=VMEM,
        scratch_shapes=[
            pltpu.VMEM((SPAN, HD), bf16),
            pltpu.VMEM((3 * SPAN, HD), bf16),
            pltpu.VMEM((3 * SPAN, 2 * HD), bf16),
            pltpu.VMEM((SPAN, HD), bf16),
        ],
        compiler_params=params(40),
        name="attend",
    )(window, span_slot, counts, *came, wide)
    attended = attended.reshape(2 * SPACE, PAIRS * ROWS, HD)
    attended = lax.all_to_all(
        attended, ("space", "head"), split_axis=0, concat_axis=0, tiled=True
    )

    tile = 512
    steps = columns // tile
    mixed = pl.pallas_call(
        project,
        grid_spec=pltpu.PrefetchScalarGridSpec(
            num_scalar_prefetch=1,
            grid=(steps,),
            in_specs=[
                pl.BlockSpec((2 * SPACE, PAIRS * ROWS, HD), lambda n, h: (0, 0, 0)),
                pl.BlockSpec((depth, tile), lambda n, h: (0, h[0] * steps + n)),
                pl.BlockSpec((depth, tile), lambda n, h: (0, n)),
            ],
            out_specs=pl.BlockSpec((SPANS * ROWS, tile), lambda n, h: (0, n)),
            scratch_shapes=[pltpu.VMEM((2, SPANS * ROWS, depth), bf16)],
        ),
        out_shape=shape((SPANS * ROWS, columns), bf16),
        compiler_params=params(32),
        name="project",
    )(half.astype(jnp.int32).reshape(1), attended, out_weight, other_weight)
    return mixed.reshape(SPANS, ROWS, columns)


def solution(mesh):
    in_specs = (
        P("cache", "space", "head"),
        P("cache", "space", "head"),
        P("cache", "space", "head"),
        P("cache", "space", "head"),
        P("cache", "space", "head"),
        P(),
        P(),
        P(),
        P("head", None),
    )
    out_specs = P("cache", "space", "head")
    return jax.shard_map(
        on_device, mesh=mesh, in_specs=in_specs, out_specs=out_specs, check_vma=False
    )
```

```python
import math

import jax
import jax.numpy as jnp
from jax import lax
from jax.experimental import pallas as pl
from jax.experimental.pallas import tpu as pltpu
from jax.sharding import PartitionSpec as P

HD = 128
WIN = 2
SPANS = 4
GROUPS = 8
SPACE = 8
ROWS = 80
SPAN = SPACE * ROWS
HEADS = 10
WIDE = SPACE * HD
PAIRS = 5
LENT_STEPS = (0, 2, 6, 4)
UNITS = 3 * PAIRS + 2 * WIN
VMEM = pl.BlockSpec(memory_space=pltpu.VMEM)
HBM = pl.BlockSpec(memory_space=pltpu.HBM)
SMEM = pl.BlockSpec(memory_space=pltpu.SMEM)
MIB = 1 << 20


def params(mib):
    return pltpu.CompilerParams(vmem_limit_bytes=mib * MIB)


def picked(window, span_slot, block, group):
    place = jnp.int32(0)
    for span in range(SPANS):
        for w in range(WIN):
            slot = span_slot[window[block * SPANS + span, w]]
            place = jnp.where((slot >> 1) == group, slot & 1, place)
    return place


def pack_slots(window, span_slot, cache_keys, cache_values, by_head, *rest):
    me = lax.axis_index("cache")
    for head in range(SPACE):
        for kv, source in enumerate((cache_keys, cache_values)):
            for slot in range(2):
                row = (kv * 2 + slot) * ROWS
                by_head[head, row : row + ROWS] = source[slot, :, head * HD : (head + 1) * HD]
    for step in range(GROUPS):
        slot = picked(window, span_slot, (me + step) & 7, me)
        for kv, source in enumerate((cache_keys, cache_values)):
            rest[step][kv] = source[slot, :, WIDE:]


def pack_all(window, span_slot, by_head, queries, keys, values, *refs):
    rest, wide_out, sent = refs[:GROUPS], refs[GROUPS], refs[GROUPS + 1 : GROUPS + 1 + SPACE]
    held, wide, pairs, wide_sems, pair_sems = refs[GROUPS + 1 + SPACE :]
    group = lax.axis_index("cache")
    me = lax.axis_index("space")
    for block in range(GROUPS):
        slot = picked(window, span_slot, block, group)
        for kv in range(2):
            for space in range(SPACE):
                row = (kv * SPACE + space) * ROWS
                start = pl.multiple_of((kv * 2 + slot) * ROWS, 16)
                wide[block, row : row + ROWS] = by_head[space, pl.ds(start, ROWS)]
        pltpu.make_async_copy(wide.at[block], wide_out.at[block], wide_sems.at[block]).start()
    for step in range(GROUPS):
        held[(group - step) & 7] = rest[step][...]
    for step in range(SPACE):
        to = (me + step) & 7
        span = to >> 1
        wide_part = pl.ds(pl.multiple_of(to * HD, HD), HD)
        last = pl.multiple_of((to & 1) * HD, HD)
        for kind, source in enumerate((queries, keys, values)):
            for pair in range(SPANS):
                pairs[step, 3 * pair + kind] = source[pair, :, wide_part]
            pairs[step, 3 * SPANS + kind] = source[
                span, :, pl.ds(pl.multiple_of(WIDE + last, HD), HD)
            ]
        for w in range(WIN):
            owner = span_slot[window[group * SPANS + span, w]] >> 1
            for kv in range(2):
                pairs[step, 3 * PAIRS + 2 * w + kv] = held[owner, kv, :, pl.ds(last, HD)]
        pltpu.make_async_copy(pairs.at[step], sent[step], pair_sems.at[step]).start()
    for block in range(GROUPS):
        pltpu.make_async_copy(wide.at[block], wide_out.at[block], wide_sems.at[block]).wait()
    for step in range(SPACE):
        pltpu.make_async_copy(pairs.at[step], sent[step], pair_sems.at[step]).wait()


def attend(window, span_slot, counts, *refs):
    came, wide, out, own, sent, k_all, v_all, done, ready, left = (refs[:SPACE],) + refs[SPACE:]
    group = lax.axis_index("cache")
    me = lax.axis_index("space")
    factor = math.log2(math.e) / math.sqrt(HD)
    spots = lax.broadcasted_iota(jnp.int32, (SPAN, HD), 0)
    v_all[0:SPAN, HD:] = jnp.ones((SPAN, HD), jnp.bfloat16)

    def fetch(pair, source, target):
        pltpu.make_async_copy(source, target, ready.at[pair]).start()

    for pair in range(PAIRS):
        for step in range(SPACE):
            rows = pl.ds(step * ROWS, ROWS)
            fetch(pair, came[step].at[pl.ds(3 * pair, 3)], own.at[pair, pl.ds(0, 3), rows])
        if pair < SPANS:
            for w in range(WIN):
                owner = span_slot[window[group * SPANS + pair, w]] >> 1
                fetch(pair, wide.at[owner], own.at[pair, pl.ds(3 + 2 * w, 2)])
        else:
            for step in range(SPACE):
                start = pl.multiple_of(((me - step) & 7) * ROWS, 16)
                fetch(
                    pair,
                    came[step].at[pl.ds(3 * PAIRS, 2 * WIN)],
                    own.at[pair, pl.ds(3, 2 * WIN), pl.ds(start, ROWS)],
                )

    @pl.loop(0, PAIRS)
    def _(pair):
        pltpu.make_async_copy(own.at[pair], own.at[pair], ready.at[pair]).wait()
        span = jnp.where(pair < SPANS, pair, me >> 1)
        k_all[0:SPAN] = own[pair, 1]
        v_all[0:SPAN, 0:HD] = own[pair, 2]
        for w in range(WIN):
            limit = counts[window[group * SPANS + span, w]]
            part = slice((1 + w) * SPAN, (2 + w) * SPAN)
            valid = spots < limit
            held = own[pair, 3 + 2 * w].astype(jnp.float32)
            first = jnp.broadcast_to(held[0:1], (SPAN, HD))
            k_all[part] = jnp.where(valid, held, first).astype(jnp.bfloat16)
            held = own[pair, 4 + 2 * w].astype(jnp.float32)
            v_all[part, 0:HD] = jnp.where(valid, held, 0.0).astype(jnp.bfloat16)
            v_all[part, HD:] = jnp.where(valid, 1.0, 0.0).astype(jnp.bfloat16)
        block = SPAN // 2
        for start in range(0, SPAN, block):
            scores = lax.dot_general(
                own[pair, 0, start : start + block],
                k_all[...],
                (((1,), (1,)), ((), ())),
                preferred_element_type=jnp.float32,
            )
            top = jnp.max(scores, axis=1, keepdims=True)
            weights = jnp.exp2((scores - top) * factor).astype(jnp.bfloat16)
            both = jnp.dot(weights, v_all[...], preferred_element_type=jnp.float32)
            done[start : start + block] = (both[:, 0:HD] / both[:, HD:]).astype(jnp.bfloat16)
        for step in range(SPACE):
            to = (me - step) & 7
            for half in range(2):
                sent[2 * to + half, pair] = done[step * ROWS : (step + 1) * ROWS]
        pltpu.make_async_copy(sent.at[:, pair], out.at[:, pair], left.at[pair]).start()

    for pair in range(PAIRS):
        pltpu.make_async_copy(sent.at[:, pair], out.at[:, pair], left.at[pair]).wait()


def project(came, own_weight, *refs):
    lent, out, features, own, other, mixed, came_sems, weight_sems, out_sems = (
        refs[:GROUPS],
        *refs[GROUPS:],
    )
    group = lax.axis_index("cache")
    half = lax.axis_index("head")
    columns = out.shape[1]
    rows = lent[0].shape[0]
    tiles = weight_sems.shape[0]
    tile = columns // tiles
    for part in range(2):
        source = half if part == 0 else 1 - half
        for space in range(SPACE):
            pltpu.make_async_copy(
                came.at[2 * space + source, pl.ds(0, SPANS * ROWS)],
                features.at[part, :, pl.ds(space * HD, HD)],
                came_sems.at[part],
            ).start()
            pltpu.make_async_copy(
                came.at[2 * space + source, pl.ds(SPANS * ROWS, ROWS)],
                features.at[
                    part, pl.ds(space // 2 * ROWS, ROWS), pl.ds(WIDE + space % 2 * HD, HD)
                ],
                came_sems.at[part],
            ).start()
    for step in range(tiles):
        here = pl.ds(step * tile, tile)
        start = pl.multiple_of(half * columns + step * tile, 128)
        pltpu.make_async_copy(
            own_weight.at[:, pl.ds(start, tile)], own.at[step], weight_sems.at[step, 0]
        ).start()
        for place, chunk in enumerate(lent):
            holder = group ^ (place // 4)
            start = pl.multiple_of(((holder - LENT_STEPS[place % 4]) & 7) * rows, 16)
            pltpu.make_async_copy(
                chunk.at[:, here], other.at[step, pl.ds(start, rows)], weight_sems.at[step, 1]
            ).start()
    for part in range(2):
        pltpu.make_async_copy(features.at[part], features.at[part], came_sems.at[part]).wait()
    for step in range(tiles):
        here = pl.ds(step * tile, tile)
        pltpu.make_async_copy(own.at[step], own.at[step], weight_sems.at[step, 0]).wait()
        total = jnp.dot(features[0], own[step], preferred_element_type=jnp.float32)
        pltpu.make_async_copy(other.at[step], other.at[step], weight_sems.at[step, 1]).wait()
        total += jnp.dot(features[1], other[step], preferred_element_type=jnp.float32)
        mixed[step] = total.astype(jnp.bfloat16)
        pltpu.make_async_copy(mixed.at[step], out.at[:, here], out_sems.at[step]).start()
    for step in range(tiles):
        here = pl.ds(step * tile, tile)
        pltpu.make_async_copy(mixed.at[step], out.at[:, here], out_sems.at[step]).wait()


def shift(x, axis, step):
    return lax.ppermute(x, axis, [(i, (i + step) % 8) for i in range(8)])


def on_device(
    queries, keys, values, cache_keys, cache_values, window, span_slot, counts, out_weight
):
    bf16 = jnp.bfloat16
    shape = jax.ShapeDtypeStruct
    group = lax.axis_index("cache")
    half = lax.axis_index("head")
    depth, width = out_weight.shape
    columns = width // 2

    rows = depth // GROUPS
    lent = lax.dynamic_slice(out_weight, (group * rows, (1 - half) * columns), (rows, columns))
    lent = lax.ppermute(lent, "head", [(0, 1), (1, 0)])

    by_head, *rest = pl.pallas_call(
        pack_slots,
        out_shape=[shape((SPACE, 4 * ROWS, HD), bf16)]
        + [shape((2, ROWS, 2 * HD), bf16)] * GROUPS,
        in_specs=[SMEM] * 2 + [VMEM] * 2,
        out_specs=[VMEM] * (1 + GROUPS),
        compiler_params=params(16),
        name="pack_slots",
    )(window, span_slot, cache_keys, cache_values)
    by_head = lax.all_to_all(by_head, "space", split_axis=0, concat_axis=0, tiled=True)
    rest = [rest[0]] + [shift(rest[step], "cache", step) for step in range(1, GROUPS)]

    lent, by_head, *rest = lax.optimization_barrier((lent, by_head, *rest))

    wide, *pairs = pl.pallas_call(
        pack_all,
        out_shape=[shape((GROUPS, 2 * SPAN, HD), bf16)] + [shape((UNITS, ROWS, HD), bf16)] * SPACE,
        in_specs=[SMEM] * 2 + [VMEM] * (4 + GROUPS),
        out_specs=[HBM] * (1 + SPACE),
        scratch_shapes=[
            pltpu.VMEM((GROUPS, 2, ROWS, 2 * HD), bf16),
            pltpu.VMEM((GROUPS, 2 * SPAN, HD), bf16),
            pltpu.VMEM((SPACE, UNITS, ROWS, HD), bf16),
            pltpu.SemaphoreType.DMA((GROUPS,)),
            pltpu.SemaphoreType.DMA((SPACE,)),
        ],
        compiler_params=params(60),
        name="pack_all",
    )(window, span_slot, by_head, queries, keys, values, *rest)
    wide = lax.all_to_all(wide, "cache", split_axis=0, concat_axis=0, tiled=True)
    came = [pairs[0]] + [shift(pairs[step], "space", step) for step in range(1, SPACE)]
    lent, wide, *came = lax.optimization_barrier((lent, wide, *came))

    lent = [lent] + [shift(lent, "cache", step) for step in LENT_STEPS[1:]]
    lent += [lax.ppermute(chunk, "cache", [(i, i ^ 1) for i in range(8)]) for chunk in lent]

    attended = pl.pallas_call(
        attend,
        out_shape=shape((2 * SPACE, PAIRS, ROWS, HD), bf16),
        in_specs=[SMEM] * 3 + [HBM] * (SPACE + 1),
        out_specs=HBM,
        scratch_shapes=[
            pltpu.VMEM((PAIRS, 3 + 2 * WIN, SPAN, HD), bf16),
            pltpu.VMEM((2 * SPACE, PAIRS, ROWS, HD), bf16),
            pltpu.VMEM((3 * SPAN, HD), bf16),
            pltpu.VMEM((3 * SPAN, 2 * HD), bf16),
            pltpu.VMEM((SPAN, HD), bf16),
            pltpu.SemaphoreType.DMA((PAIRS,)),
            pltpu.SemaphoreType.DMA((PAIRS,)),
        ],
        compiler_params=params(60),
        name="attend",
    )(window, span_slot, counts, *came, wide.reshape(GROUPS, 2, SPAN, HD))
    attended = attended.reshape(2 * SPACE, PAIRS * ROWS, HD)
    attended = lax.all_to_all(
        attended, ("space", "head"), split_axis=0, concat_axis=0, tiled=True
    )

    tile = 512
    tiles = columns // tile
    mixed = pl.pallas_call(
        project,
        out_shape=shape((SPANS * ROWS, columns), bf16),
        in_specs=[HBM] * (2 + GROUPS),
        out_specs=HBM,
        scratch_shapes=[
            pltpu.VMEM((2, SPANS * ROWS, depth), bf16),
            pltpu.VMEM((tiles, depth, tile), bf16),
            pltpu.VMEM((tiles, depth, tile), bf16),
            pltpu.VMEM((tiles, SPANS * ROWS, tile), bf16),
            pltpu.SemaphoreType.DMA((2,)),
            pltpu.SemaphoreType.DMA((tiles, 2)),
            pltpu.SemaphoreType.DMA((tiles,)),
        ],
        compiler_params=params(60),
        name="project",
    )(attended, out_weight, *lent)
    return mixed.reshape(SPANS, ROWS, columns)


def solution(mesh):
    in_specs = (
        P("cache", "space", "head"),
        P("cache", "space", "head"),
        P("cache", "space", "head"),
        P("cache", "space", "head"),
        P("cache", "space", "head"),
        P(),
        P(),
        P(),
        P("head", None),
    )
    out_specs = P("cache", "space", "head")
    return jax.shard_map(
        on_device, mesh=mesh, in_specs=in_specs, out_specs=out_specs, check_vma=False
    )
```

```python
import math

import jax
import jax.numpy as jnp
from jax import lax
from jax.experimental import pallas as pl
from jax.experimental.pallas import tpu as pltpu
from jax.sharding import PartitionSpec as P

HD = 128
WIN = 2
SPANS = 4
GROUPS = 8
SPACE = 8
ROWS = 80
SPAN = SPACE * ROWS
HEADS = 10
WIDE = SPACE * HD
PAIRS = 5
LENT = (0, 2, 3, 4)
UNITS = 3 * PAIRS + 2 * WIN
AHEAD = 2
STEPS = ((0, 0), (0, 1), (1, 0), (3, 0), (2, 0), (1, 1), (3, 1), (2, 1))
VMEM = pl.BlockSpec(memory_space=pltpu.VMEM)
HBM = pl.BlockSpec(memory_space=pltpu.HBM)
SMEM = pl.BlockSpec(memory_space=pltpu.SMEM)
MIB = 1 << 20


def params(mib):
    return pltpu.CompilerParams(vmem_limit_bytes=mib * MIB)


def goes_to(me, step):
    ring, cross = STEPS[step]
    return ((((me >> 1) + ring) & 3) << 1) | ((me & 1) ^ cross)


def came_from(me, step):
    ring, cross = STEPS[step]
    return ((((me >> 1) - ring) & 3) << 1) | ((me & 1) ^ cross)


def shift(x, axis, step):
    return lax.ppermute(x, axis, [(i, goes_to(i, step)) for i in range(8)])


def wait_for(ref, sem):
    pltpu.make_async_copy(ref, ref, sem).wait()


def picked(window, span_slot, block, group):
    place = jnp.int32(0)
    for span in range(SPANS):
        for w in range(WIN):
            slot = span_slot[window[w, block * SPANS + span]]
            place = jnp.where((slot >> 1) == group, slot & 1, place)
    return place


def pack_slots(window, span_slot, cache_keys, cache_values, by_head, *refs):
    rest, held, held_sems, sems = refs[:GROUPS], *refs[GROUPS:]
    me = lax.axis_index("cache")
    for kv, source in enumerate((cache_keys, cache_values)):
        pltpu.make_async_copy(source, held.at[kv], held_sems.at[kv]).start()
    for kv, source in enumerate((cache_keys, cache_values)):
        pltpu.make_async_copy(source, held.at[kv], held_sems.at[kv]).wait()
    for head in range(SPACE):
        source = held.at[:, :, :, pl.ds(head * HD, HD)]
        pltpu.make_async_copy(source, by_head.at[head], sems.at[0]).start()
    for step in range(GROUPS):
        slot = picked(window, span_slot, goes_to(me, step), me)
        source = held.at[:, slot, :, pl.ds(WIDE, 2 * HD)]
        pltpu.make_async_copy(source, rest[step], sems.at[1 + step]).start()
    wait_for(by_head, sems.at[0])
    for step in range(GROUPS):
        wait_for(rest[step], sems.at[1 + step])


def pack_pairs(queries, keys, values, out_weight, sent, *refs):
    lent, held, rows_held, held_sems, sems = refs[:2], *refs[2:]
    rows, columns = lent[0].shape
    column = pl.multiple_of((1 - lax.axis_index("head")) * columns, HD)
    loads = [
        pltpu.make_async_copy(source, held.at[kind], held_sems.at[kind])
        for kind, source in enumerate((queries, keys, values))
    ]
    for part in range(2):
        row = pl.multiple_of((2 * lax.axis_index("cache") + part) * rows, 16)
        source = out_weight.at[pl.ds(row, rows), pl.ds(column, columns)]
        loads.append(pltpu.make_async_copy(source, rows_held.at[part], held_sems.at[3 + part]))
    for load in loads:
        load.start()
    for kind in range(3):
        loads[kind].wait()
        for to in range(SPACE):
            wide, last = pl.ds(to * HD, HD), pl.ds(WIDE + to % 2 * HD, HD)
            pltpu.make_async_copy(
                held.at[kind, :, :, wide], sent.at[to, pl.ds(kind * PAIRS, SPANS)], sems.at[kind]
            ).start()
            pltpu.make_async_copy(
                held.at[kind, to // 2, :, last], sent.at[to, kind * PAIRS + SPANS], sems.at[kind]
            ).start()
    for part in range(2):
        loads[3 + part].wait()
        pltpu.make_async_copy(rows_held.at[part], lent[part], sems.at[3 + part]).start()
    for kind in range(3):
        wait_for(sent.at[:, pl.ds(kind * PAIRS, PAIRS)], sems.at[kind])
    for part in range(2):
        wait_for(lent[part], sems.at[3 + part])


def pack_cached(window, span_slot, by_head, *refs):
    rest, sent, wide = refs[:GROUPS], refs[GROUPS + 1], refs[GROUPS + 2 : 2 * GROUPS + 2]
    held, heads, held_sems, wide_sems, sent_sem = refs[2 * GROUPS + 2 :]
    group = lax.axis_index("cache")
    loads = [pltpu.make_async_copy(by_head, heads, held_sems.at[GROUPS])]
    for step in range(GROUPS):
        target = held.at[came_from(group, step)]
        loads.append(pltpu.make_async_copy(rest[step], target, held_sems.at[step]))
    for load in loads:
        load.start()
    loads[0].wait()
    for step in range(GROUPS):
        slot = picked(window, span_slot, goes_to(group, step), group)
        for kv in range(2):
            source = heads.at[:, kv, slot]
            pltpu.make_async_copy(source, wide[step].at[kv], wide_sems.at[step]).start()
    for load in loads[1:]:
        load.wait()
    for to in range(SPACE):
        for w in range(WIN):
            owner = span_slot[window[w, group * SPANS + to // 2]] >> 1
            pltpu.make_async_copy(
                held.at[owner, :, :, pl.ds(to % 2 * HD, HD)],
                sent.at[to, pl.ds(3 * PAIRS + 2 * w, 2)],
                sent_sem.at[0],
            ).start()
    for step in range(GROUPS):
        wait_for(wide[step], wide_sems.at[step])
    wait_for(sent.at[:, pl.ds(3 * PAIRS, 2 * WIN)], sent_sem.at[0])


def attend(window, span_slot, counts, *refs):
    came, wide = refs[0], refs[1 : 1 + GROUPS]
    out, own, sent, k_all, v_all, done, ready, left = refs[1 + GROUPS :]
    group = lax.axis_index("cache")
    me = lax.axis_index("space")
    factor = math.log2(math.e) / math.sqrt(HD)
    spots = lax.broadcasted_iota(jnp.int32, (SPAN, HD), 0)
    v_all[0:SPAN, HD:] = jnp.ones((SPAN, HD), jnp.bfloat16)

    def fetch(pair, source, target):
        pltpu.make_async_copy(source, target, ready.at[pair]).start()

    def fetch_pair(pair):
        for kind in range(3):
            fetch(pair, came.at[:, kind * PAIRS + pair], own.at[pair, kind])

    fetch_pair(0)
    for step in range(GROUPS):
        owner = came_from(group, step)
        place = jnp.int32(0)
        for entry in range(SPANS * WIN):
            slot = span_slot[window[entry % 2, group * SPANS + entry // 2]]
            place = jnp.where((slot >> 1) == owner, entry, place)
        fetch(place >> 1, wide[step], own.at[place >> 1, pl.ds(3 + 2 * (place & 1), 2)])
    for pair in range(1, PAIRS):
        fetch_pair(pair)
    for unit in range(2 * WIN):
        fetch(SPANS, came.at[:, 3 * PAIRS + unit], own.at[SPANS, 3 + unit])

    @pl.loop(0, PAIRS)
    def _(pair):
        pltpu.make_async_copy(own.at[pair], own.at[pair], ready.at[pair]).wait()
        span = jnp.where(pair < SPANS, pair, me >> 1)
        k_all[0:SPAN] = own[pair, 1].reshape(SPAN, HD)
        v_all[0:SPAN, 0:HD] = own[pair, 2].reshape(SPAN, HD)
        for w in range(WIN):
            limit = counts[window[w, group * SPANS + span]]
            part = slice((1 + w) * SPAN, (2 + w) * SPAN)
            valid = spots < limit
            held = own[pair, 3 + 2 * w].reshape(SPAN, HD).astype(jnp.float32)
            first = jnp.broadcast_to(held[0:1], (SPAN, HD))
            k_all[part] = jnp.where(valid, held, first).astype(jnp.bfloat16)
            held = own[pair, 4 + 2 * w].reshape(SPAN, HD).astype(jnp.float32)
            v_all[part, 0:HD] = jnp.where(valid, held, 0.0).astype(jnp.bfloat16)
            v_all[part, HD:] = jnp.where(valid, 1.0, 0.0).astype(jnp.bfloat16)
        share = SPACE // 2
        block = share * ROWS
        for first in range(0, SPACE, share):
            start = first * ROWS
            scores = lax.dot_general(
                own[pair, 0, first : first + share].reshape(block, HD),
                k_all[...],
                (((1,), (1,)), ((), ())),
                preferred_element_type=jnp.float32,
            )
            top = jnp.max(scores, axis=1, keepdims=True)
            weights = jnp.exp2((scores - top) * factor).astype(jnp.bfloat16)
            both = jnp.dot(weights, v_all[...], preferred_element_type=jnp.float32)
            done[start : start + block] = (both[:, 0:HD] / both[:, HD:]).astype(jnp.bfloat16)
        for step in range(SPACE):
            for half in range(2):
                sent[2 * step + half, pair] = done[step * ROWS : (step + 1) * ROWS]
        pltpu.make_async_copy(sent.at[:, pair], out.at[:, pair], left.at[pair]).start()

    for pair in range(PAIRS):
        pltpu.make_async_copy(sent.at[:, pair], out.at[:, pair], left.at[pair]).wait()


def project(came, own_weight, *refs):
    lent, out, features, own, other, mixed, came_sems, weight_sems, out_sems = (
        refs[:GROUPS],
        *refs[GROUPS:],
    )
    group = lax.axis_index("cache")
    half = lax.axis_index("head")
    columns = out.shape[1]
    rows = lent[0].shape[0]
    tiles = weight_sems.shape[0]
    tile = columns // tiles
    for part in range(2):
        source = half if part == 0 else 1 - half
        for space in range(SPACE):
            pltpu.make_async_copy(
                came.at[2 * space + source, pl.ds(0, SPANS * ROWS)],
                features.at[part, :, pl.ds(space * HD, HD)],
                came_sems.at[part],
            ).start()
            pltpu.make_async_copy(
                came.at[2 * space + source, pl.ds(SPANS * ROWS, ROWS)],
                features.at[
                    part, pl.ds(space // 2 * ROWS, ROWS), pl.ds(WIDE + space % 2 * HD, HD)
                ],
                came_sems.at[part],
            ).start()

    def fetch(step):
        here = pl.ds(step * tile, tile)
        start = pl.multiple_of(half * columns + step * tile, 128)
        pltpu.make_async_copy(
            own_weight.at[:, pl.ds(start, tile)], own.at[step], weight_sems.at[step, 0]
        ).start()
        for place, chunk in enumerate(lent):
            holder = group ^ (place // 4)
            start = pl.multiple_of(came_from(holder, LENT[place % 4]) * rows, 16)
            pltpu.make_async_copy(
                chunk.at[:, here], other.at[step, pl.ds(start, rows)], weight_sems.at[step, 1]
            ).start()

    for step in range(AHEAD):
        fetch(step)
    for part in range(2):
        wait_for(features.at[part], came_sems.at[part])
    for step in range(tiles):
        here = pl.ds(step * tile, tile)
        wait_for(own.at[step], weight_sems.at[step, 0])
        wait_for(other.at[step], weight_sems.at[step, 1])
        if step + AHEAD < tiles:
            fetch(step + AHEAD)
        total = jnp.dot(features[0], own[step], preferred_element_type=jnp.float32)
        total += jnp.dot(features[1], other[step], preferred_element_type=jnp.float32)
        mixed[step] = total.astype(jnp.bfloat16)
        pltpu.make_async_copy(mixed.at[step], out.at[:, here], out_sems.at[step]).start()
    for step in range(tiles):
        here = pl.ds(step * tile, tile)
        pltpu.make_async_copy(mixed.at[step], out.at[:, here], out_sems.at[step]).wait()


def on_device(
    queries, keys, values, cache_keys, cache_values, window, span_slot, counts, out_weight
):
    bf16 = jnp.bfloat16
    shape = jax.ShapeDtypeStruct
    depth, width = out_weight.shape
    columns = width // 2

    rows = depth // GROUPS // 2
    window = window.T

    by_head, *rest = pl.pallas_call(
        pack_slots,
        out_shape=[shape((SPACE, 2, 2, ROWS, HD), bf16)]
        + [shape((2, ROWS, 2 * HD), bf16)] * GROUPS,
        in_specs=[SMEM] * 2 + [HBM] * 2,
        out_specs=[HBM] * (1 + GROUPS),
        scratch_shapes=[
            pltpu.VMEM((2, 2, ROWS, HEADS * HD), bf16),
            pltpu.SemaphoreType.DMA((2,)),
            pltpu.SemaphoreType.DMA((1 + GROUPS,)),
        ],
        compiler_params=params(60),
        name="pack_slots",
    )(window, span_slot, cache_keys, cache_values)
    by_head, *rest, queries = lax.optimization_barrier((by_head, *rest, queries))
    by_head = lax.all_to_all(
        by_head.reshape(SPACE, 4 * ROWS, HD), "space", split_axis=0, concat_axis=0, tiled=True
    ).reshape(by_head.shape)
    rest = [rest[0]] + [shift(rest[step], "cache", step) for step in range(1, GROUPS)]

    pairs, *lent = pl.pallas_call(
        pack_pairs,
        out_shape=[shape((SPACE, UNITS, ROWS, HD), bf16)] + [shape((rows, columns), bf16)] * 2,
        in_specs=[HBM] * 4,
        out_specs=[HBM] * 3,
        scratch_shapes=[
            pltpu.VMEM((3, SPANS, ROWS, HEADS * HD), bf16),
            pltpu.VMEM((2, rows, columns), bf16),
            pltpu.SemaphoreType.DMA((5,)),
            pltpu.SemaphoreType.DMA((5,)),
        ],
        compiler_params=params(60),
        name="pack_pairs",
    )(queries, keys, values, out_weight)
    lent = [
        lax.ppermute(lent[0], "head", [(0, 1), (1, 0)]),
        lax.ppermute(lent[1], ("space", "head"), [(i, i ^ 3) for i in range(2 * SPACE)]),
    ]
    lent = jnp.concatenate(lent, 0)
    by_head, lent, *rest = lax.optimization_barrier((by_head, lent, *rest))
    pairs, *wide = pl.pallas_call(
        pack_cached,
        out_shape=[shape(pairs.shape, bf16)] + [shape((2, SPACE, ROWS, HD), bf16)] * GROUPS,
        in_specs=[SMEM] * 2 + [HBM] * (2 + GROUPS),
        out_specs=[HBM] * (1 + GROUPS),
        input_output_aliases={3 + GROUPS: 0},
        scratch_shapes=[
            pltpu.VMEM((GROUPS, 2, ROWS, 2 * HD), bf16),
            pltpu.VMEM(by_head.shape, bf16),
            pltpu.SemaphoreType.DMA((GROUPS + 1,)),
            pltpu.SemaphoreType.DMA((GROUPS,)),
            pltpu.SemaphoreType.DMA((1,)),
        ],
        compiler_params=params(60),
        name="pack_cached",
    )(window, span_slot, by_head, *rest, pairs)
    came = lax.all_to_all(
        pairs.reshape(SPACE, UNITS * ROWS, HD), "space", split_axis=0, concat_axis=0, tiled=True
    ).reshape(pairs.shape)
    wide = [wide[0]] + [shift(wide[step], "cache", step) for step in range(1, GROUPS)]
    came, lent, *wide = lax.optimization_barrier((came, lent, *wide))
    lent = [lent] + [shift(lent, "cache", step) for step in LENT[1:]]
    lent += [lax.ppermute(chunk, "cache", [(i, i ^ 1) for i in range(8)]) for chunk in lent]

    attended = pl.pallas_call(
        attend,
        out_shape=shape((2 * SPACE, PAIRS, ROWS, HD), bf16),
        in_specs=[SMEM] * 3 + [HBM] * (1 + GROUPS),
        out_specs=HBM,
        scratch_shapes=[
            pltpu.VMEM((PAIRS, 3 + 2 * WIN, SPACE, ROWS, HD), bf16),
            pltpu.VMEM((2 * SPACE, PAIRS, ROWS, HD), bf16),
            pltpu.VMEM((3 * SPAN, HD), bf16),
            pltpu.VMEM((3 * SPAN, 2 * HD), bf16),
            pltpu.VMEM((SPAN, HD), bf16),
            pltpu.SemaphoreType.DMA((PAIRS,)),
            pltpu.SemaphoreType.DMA((PAIRS,)),
        ],
        compiler_params=params(60),
        name="attend",
    )(window, span_slot, counts, came, *wide)
    attended = attended.reshape(2 * SPACE, PAIRS * ROWS, HD)
    attended = lax.all_to_all(
        attended, ("space", "head"), split_axis=0, concat_axis=0, tiled=True
    )

    tile = 512
    tiles = columns // tile
    mixed = pl.pallas_call(
        project,
        out_shape=shape((SPANS * ROWS, columns), bf16),
        in_specs=[HBM] * (2 + GROUPS),
        out_specs=HBM,
        scratch_shapes=[
            pltpu.VMEM((2, SPANS * ROWS, depth), bf16),
            pltpu.VMEM((tiles, depth, tile), bf16),
            pltpu.VMEM((tiles, depth, tile), bf16),
            pltpu.VMEM((tiles, SPANS * ROWS, tile), bf16),
            pltpu.SemaphoreType.DMA((2,)),
            pltpu.SemaphoreType.DMA((tiles, 2)),
            pltpu.SemaphoreType.DMA((tiles,)),
        ],
        compiler_params=params(52),
        name="project",
    )(attended, out_weight, *lent)
    return mixed.reshape(SPANS, ROWS, columns)


def solution(mesh):
    in_specs = (
        P("cache", "space", "head"),
        P("cache", "space", "head"),
        P("cache", "space", "head"),
        P("cache", "space", "head"),
        P("cache", "space", "head"),
        P(),
        P(),
        P(),
        P("head", None),
    )
    out_specs = P("cache", "space", "head")
    return jax.shard_map(
        on_device, mesh=mesh, in_specs=in_specs, out_specs=out_specs, check_vma=False
    )
```

```python
import math

import jax
import jax.numpy as jnp
from jax import lax
from jax.experimental import pallas as pl
from jax.experimental.pallas import tpu as pltpu
from jax.sharding import PartitionSpec as P

HD = 128
WIN = 2
SPANS = 4
GROUPS = 8
SPACE = 8
ROWS = 80
SPAN = SPACE * ROWS
HEADS = 10
WIDE = SPACE * HD
PAIRS = 5
LENT = (0, 2, 3, 4)
UNITS = 3 * PAIRS + 2 * WIN
BLOCKS = 4
AHEAD = 2
STEPS = ((0, 0), (0, 1), (1, 0), (3, 0), (2, 0), (1, 1), (3, 1), (2, 1))
VMEM = pl.BlockSpec(memory_space=pltpu.VMEM)
HBM = pl.BlockSpec(memory_space=pltpu.HBM)
SMEM = pl.BlockSpec(memory_space=pltpu.SMEM)
MIB = 1 << 20


def params(mib):
    return pltpu.CompilerParams(vmem_limit_bytes=mib * MIB)


def goes_to(me, step):
    ring, cross = STEPS[step]
    return ((((me >> 1) + ring) & 3) << 1) | ((me & 1) ^ cross)


def came_from(me, step):
    ring, cross = STEPS[step]
    return ((((me >> 1) - ring) & 3) << 1) | ((me & 1) ^ cross)


def shift(x, axis, step):
    return lax.ppermute(x, axis, [(i, goes_to(i, step)) for i in range(8)])


def wait_for(ref, sem):
    pltpu.make_async_copy(ref, ref, sem).wait()


def picked(window, span_slot, block, group):
    place = jnp.int32(0)
    for span in range(SPANS):
        for w in range(WIN):
            slot = span_slot[window[w, block * SPANS + span]]
            place = jnp.where((slot >> 1) == group, slot & 1, place)
    return place


def pack_slots(window, span_slot, cache_keys, cache_values, out_weight, by_head, *refs):
    rest, lent = refs[:GROUPS], refs[GROUPS : GROUPS + 2]
    held, lent_held, held_sems, sems = refs[GROUPS + 2 :]
    me = lax.axis_index("cache")
    rows, columns = lent[0].shape
    column = pl.multiple_of((1 - lax.axis_index("head")) * columns, HD)
    for kv, source in enumerate((cache_keys, cache_values)):
        pltpu.make_async_copy(source, held.at[kv], held_sems.at[kv]).start()
    loads = []
    for part in range(2):
        row = pl.multiple_of((2 * me + part) * rows, 16)
        source = out_weight.at[pl.ds(row, rows), pl.ds(column, columns)]
        loads.append(pltpu.make_async_copy(source, lent_held.at[part], held_sems.at[2 + part]))
        loads[part].start()
    for kv, source in enumerate((cache_keys, cache_values)):
        pltpu.make_async_copy(source, held.at[kv], held_sems.at[kv]).wait()
    for head in range(SPACE):
        source = held.at[:, :, :, pl.ds(head * HD, HD)]
        pltpu.make_async_copy(source, by_head.at[head], sems.at[0]).start()
    for step in range(GROUPS):
        slot = picked(window, span_slot, goes_to(me, step), me)
        source = held.at[:, slot, :, pl.ds(WIDE, 2 * HD)]
        pltpu.make_async_copy(source, rest[step], sems.at[1 + step]).start()
    for part in range(2):
        loads[part].wait()
        pltpu.make_async_copy(lent_held.at[part], lent[part], sems.at[1 + GROUPS + part]).start()
    wait_for(by_head, sems.at[0])
    for part in range(2):
        wait_for(lent[part], sems.at[1 + GROUPS + part])
    for step in range(GROUPS):
        wait_for(rest[step], sems.at[1 + step])


def pack_pairs(queries, keys, values, sent, held, held_sems, sems):
    loads = [
        pltpu.make_async_copy(source, held.at[kind], held_sems.at[kind])
        for kind, source in enumerate((queries, keys, values))
    ]
    for load in loads:
        load.start()
    for kind in range(3):
        loads[kind].wait()
        for to in range(SPACE):
            wide, last = pl.ds(to * HD, HD), pl.ds(WIDE + to % 2 * HD, HD)
            pltpu.make_async_copy(
                held.at[kind, :, :, wide], sent.at[to, pl.ds(kind * PAIRS, SPANS)], sems.at[kind]
            ).start()
            pltpu.make_async_copy(
                held.at[kind, to // 2, :, last], sent.at[to, kind * PAIRS + SPANS], sems.at[kind]
            ).start()
    for kind in range(3):
        wait_for(sent.at[:, pl.ds(kind * PAIRS, PAIRS)], sems.at[kind])


def pack_cached(window, span_slot, by_head, *refs):
    rest, sent, wide = refs[:GROUPS], refs[GROUPS + 1], refs[GROUPS + 2 : 2 * GROUPS + 2]
    held, heads, held_sems, wide_sems, sent_sem = refs[2 * GROUPS + 2 :]
    group = lax.axis_index("cache")
    loads = [pltpu.make_async_copy(by_head, heads, held_sems.at[GROUPS])]
    for step in range(GROUPS):
        target = held.at[came_from(group, step)]
        loads.append(pltpu.make_async_copy(rest[step], target, held_sems.at[step]))
    for load in loads:
        load.start()
    loads[0].wait()
    for step in range(GROUPS):
        slot = picked(window, span_slot, goes_to(group, step), group)
        for kv in range(2):
            source = heads.at[:, kv, slot]
            pltpu.make_async_copy(source, wide[step].at[kv], wide_sems.at[step]).start()
    for load in loads[1:]:
        load.wait()
    for to in range(SPACE):
        for w in range(WIN):
            owner = span_slot[window[w, group * SPANS + to // 2]] >> 1
            pltpu.make_async_copy(
                held.at[owner, :, :, pl.ds(to % 2 * HD, HD)],
                sent.at[to, pl.ds(3 * PAIRS + 2 * w, 2)],
                sent_sem.at[0],
            ).start()
    for step in range(GROUPS):
        wait_for(wide[step], wide_sems.at[step])
    wait_for(sent.at[:, pl.ds(3 * PAIRS, 2 * WIN)], sent_sem.at[0])


def attend(window, span_slot, counts, *refs):
    came, wide = refs[0], refs[1 : 1 + GROUPS]
    out, q_all, k_all, v_all, sent, ready, left = refs[1 + GROUPS :]
    group = lax.axis_index("cache")
    me = lax.axis_index("space")
    factor = math.log2(math.e) / math.sqrt(HD)

    def fetch(pair, kind, source, target):
        pltpu.make_async_copy(source, target, ready.at[pair, kind]).start()

    def share(pair, kind, segment):
        if kind == 0:
            return q_all.at[pair]
        chunks = pl.ds(segment * SPACE, SPACE)
        if kind == 1:
            return k_all.at[pair, chunks]
        return v_all.at[pair, chunks, :, pl.ds(0, HD)]

    def fetch_pair(pair):
        for kind in range(3):
            fetch(pair, kind, came.at[:, kind * PAIRS + pair], share(pair, kind, 0))

    def fetch_wide(step, place):
        pair, segment = place >> 1, 1 + (place & 1)
        for kv in range(2):
            fetch(pair, 1 + kv, wide[step].at[kv], share(pair, 1 + kv, segment))

    fetch_pair(0)
    places = []
    for step in range(GROUPS):
        owner = came_from(group, step)
        place = jnp.int32(0)
        for entry in range(SPANS * WIN):
            slot = span_slot[window[entry % 2, group * SPANS + entry // 2]]
            place = jnp.where((slot >> 1) == owner, entry, place)
        places.append(place)
        pl.when(place < WIN)(lambda: fetch_wide(step, place))
    v_all[:, :, :, HD:] = jnp.ones((PAIRS, 3 * SPACE, ROWS, HD), jnp.bfloat16)

    def prepare(pair):
        for kind in range(3):
            wait_for(q_all.at[pair] if kind == 0 else k_all.at[pair], ready.at[pair, kind])
        span = me >> 1 if pair == SPANS else pair
        for w in range(WIN):
            limit = counts[window[w, group * SPANS + span]]
            first = (1 + w) * SPACE
            half = slice(first + SPACE // 2, first + SPACE)
            extent = (SPACE // 2, ROWS, HD)
            spots = SPAN // 2 + lax.broadcasted_iota(jnp.int32, extent, 1)
            valid = spots + ROWS * lax.broadcasted_iota(jnp.int32, extent, 0) < limit
            key = k_all[pair, first, 0:1].astype(jnp.float32)
            key = jnp.broadcast_to(key[None], extent)
            held = k_all[pair, half].astype(jnp.float32)
            k_all[pair, half] = jnp.where(valid, held, key).astype(jnp.bfloat16)
            held = v_all[pair, half, :, 0:HD].astype(jnp.float32)
            v_all[pair, half, :, 0:HD] = jnp.where(valid, held, 0.0).astype(jnp.bfloat16)
            v_all[pair, half, :, HD:] = jnp.where(valid, 1.0, 0.0).astype(jnp.bfloat16)

    block = SPACE // BLOCKS

    def score(pair, part):
        query = q_all[pair, part * block : (part + 1) * block].reshape(block * ROWS, HD)
        key = k_all[pair].reshape(3 * SPAN, HD)
        return lax.dot_general(
            query, key, (((1,), (1,)), ((), ())), preferred_element_type=jnp.float32
        )

    def finish(pair, part, scores):
        top = jnp.max(scores, axis=1, keepdims=True)
        weights = jnp.exp2((scores - top) * factor).astype(jnp.bfloat16)
        value = v_all[pair].reshape(3 * SPAN, 2 * HD)
        both = jnp.dot(weights, value, preferred_element_type=jnp.float32)
        done = (both[:, 0:HD] / both[:, HD:]).astype(jnp.bfloat16).reshape(block, ROWS, HD)
        for place in range(block):
            for half in range(2):
                sent[2 * (part * block + place) + half, pair] = done[place]

    steps = [(pair, part) for pair in range(PAIRS) for part in range(BLOCKS)]
    prepare(0)
    for step, place in enumerate(places):
        pl.when(place >= WIN)(lambda: fetch_wide(step, place))
    for pair in range(1, PAIRS):
        fetch_pair(pair)
    for w in range(WIN):
        for kv in range(2):
            source = came.at[:, 3 * PAIRS + 2 * w + kv]
            fetch(SPANS, 1 + kv, source, share(SPANS, 1 + kv, 1 + w))
    scores = score(0, 0)
    for now, later in zip(steps, steps[1:] + [None]):
        held = scores
        if later is not None:
            if later[1] == 0:
                prepare(later[0])
            scores = score(*later)
        finish(*now, held)
        if now[1] == BLOCKS - 1:
            pair = now[0]
            pltpu.make_async_copy(sent.at[:, pair], out.at[:, pair], left.at[pair]).start()

    for pair in range(PAIRS):
        pltpu.make_async_copy(sent.at[:, pair], out.at[:, pair], left.at[pair]).wait()


def project(came, own_weight, *refs):
    lent, out, features, own, other, mixed, came_sems, weight_sems, out_sems = (
        refs[:GROUPS],
        *refs[GROUPS:],
    )
    group = lax.axis_index("cache")
    half = lax.axis_index("head")
    columns = out.shape[1]
    rows = lent[0].shape[0]
    tiles = weight_sems.shape[0]
    tile = columns // tiles
    for part in range(2):
        source = half if part == 0 else 1 - half
        for space in range(SPACE):
            pltpu.make_async_copy(
                came.at[2 * space + source, pl.ds(0, SPANS * ROWS)],
                features.at[part, :, pl.ds(space * HD, HD)],
                came_sems.at[part],
            ).start()
            pltpu.make_async_copy(
                came.at[2 * space + source, pl.ds(SPANS * ROWS, ROWS)],
                features.at[
                    part, pl.ds(space // 2 * ROWS, ROWS), pl.ds(WIDE + space % 2 * HD, HD)
                ],
                came_sems.at[part],
            ).start()

    def fetch(step):
        here = pl.ds(step * tile, tile)
        start = pl.multiple_of(half * columns + step * tile, 128)
        pltpu.make_async_copy(
            own_weight.at[:, pl.ds(start, tile)], own.at[step], weight_sems.at[step, 0]
        ).start()
        for place, chunk in enumerate(lent):
            holder = group ^ (place // 4)
            start = pl.multiple_of(came_from(holder, LENT[place % 4]) * rows, 16)
            pltpu.make_async_copy(
                chunk.at[:, here], other.at[step, pl.ds(start, rows)], weight_sems.at[step, 1]
            ).start()

    for step in range(AHEAD):
        fetch(step)
    for part in range(2):
        wait_for(features.at[part], came_sems.at[part])
    for step in range(tiles):
        here = pl.ds(step * tile, tile)
        wait_for(own.at[step], weight_sems.at[step, 0])
        wait_for(other.at[step], weight_sems.at[step, 1])
        if step + AHEAD < tiles:
            fetch(step + AHEAD)
        total = jnp.dot(features[0], own[step], preferred_element_type=jnp.float32)
        total += jnp.dot(features[1], other[step], preferred_element_type=jnp.float32)
        mixed[step] = total.astype(jnp.bfloat16)
        pltpu.make_async_copy(mixed.at[step], out.at[:, here], out_sems.at[step]).start()
    for step in range(tiles):
        here = pl.ds(step * tile, tile)
        pltpu.make_async_copy(mixed.at[step], out.at[:, here], out_sems.at[step]).wait()


def on_device(
    queries, keys, values, cache_keys, cache_values, window, span_slot, counts, out_weight
):
    bf16 = jnp.bfloat16
    shape = jax.ShapeDtypeStruct
    depth, width = out_weight.shape
    columns = width // 2

    rows = depth // GROUPS // 2
    window = window.T

    by_head, *sent = pl.pallas_call(
        pack_slots,
        out_shape=[shape((SPACE, 2, 2, ROWS, HD), bf16)]
        + [shape((2, ROWS, 2 * HD), bf16)] * GROUPS
        + [shape((rows, columns), bf16)] * 2,
        in_specs=[SMEM] * 2 + [HBM] * 3,
        out_specs=[HBM] * (3 + GROUPS),
        scratch_shapes=[
            pltpu.VMEM((2, 2, ROWS, HEADS * HD), bf16),
            pltpu.VMEM((2, rows, columns), bf16),
            pltpu.SemaphoreType.DMA((4,)),
            pltpu.SemaphoreType.DMA((3 + GROUPS,)),
        ],
        compiler_params=params(60),
        name="pack_slots",
    )(window, span_slot, cache_keys, cache_values, out_weight)
    by_head, *sent, queries = lax.optimization_barrier((by_head, *sent, queries))
    rest, lent = sent[:GROUPS], sent[GROUPS:]
    by_head = lax.all_to_all(
        by_head.reshape(SPACE, 4 * ROWS, HD), "space", split_axis=0, concat_axis=0, tiled=True
    ).reshape(by_head.shape)
    rest = [rest[0]] + [shift(rest[step], "cache", step) for step in range(1, GROUPS)]
    lent = [
        lax.ppermute(lent[0], "head", [(0, 1), (1, 0)]),
        lax.ppermute(lent[1], ("space", "head"), [(i, i ^ 3) for i in range(2 * SPACE)]),
    ]
    pairs = pl.pallas_call(
        pack_pairs,
        out_shape=shape((SPACE, UNITS, ROWS, HD), bf16),
        in_specs=[HBM] * 3,
        out_specs=HBM,
        scratch_shapes=[
            pltpu.VMEM((3, SPANS, ROWS, HEADS * HD), bf16),
            pltpu.SemaphoreType.DMA((3,)),
            pltpu.SemaphoreType.DMA((3,)),
        ],
        compiler_params=params(60),
        name="pack_pairs",
    )(queries, keys, values)
    by_head, *rest = lax.optimization_barrier((by_head, *rest))
    pairs, *wide = pl.pallas_call(
        pack_cached,
        out_shape=[shape(pairs.shape, bf16)] + [shape((2, SPACE, ROWS, HD), bf16)] * GROUPS,
        in_specs=[SMEM] * 2 + [HBM] * (2 + GROUPS),
        out_specs=[HBM] * (1 + GROUPS),
        input_output_aliases={3 + GROUPS: 0},
        scratch_shapes=[
            pltpu.VMEM((GROUPS, 2, ROWS, 2 * HD), bf16),
            pltpu.VMEM(by_head.shape, bf16),
            pltpu.SemaphoreType.DMA((GROUPS + 1,)),
            pltpu.SemaphoreType.DMA((GROUPS,)),
            pltpu.SemaphoreType.DMA((1,)),
        ],
        compiler_params=params(60),
        name="pack_cached",
    )(window, span_slot, by_head, *rest, pairs)
    pairs, *lent = lax.optimization_barrier((pairs, *lent))
    came = lax.all_to_all(
        pairs.reshape(SPACE, UNITS * ROWS, HD), "space", split_axis=0, concat_axis=0, tiled=True
    ).reshape(pairs.shape)
    wide = [wide[0]] + [shift(wide[step], "cache", step) for step in range(1, GROUPS)]
    lent = jnp.concatenate(lent, 0)
    lent, *wide = lax.optimization_barrier((lent, *wide))
    lent = [lent] + [shift(lent, "cache", step) for step in LENT[1:]]
    lent += [lax.ppermute(chunk, "cache", [(i, i ^ 1) for i in range(8)]) for chunk in lent]

    attended = pl.pallas_call(
        attend,
        out_shape=shape((2 * SPACE, PAIRS, ROWS, HD), bf16),
        in_specs=[SMEM] * 3 + [HBM] * (1 + GROUPS),
        out_specs=HBM,
        scratch_shapes=[
            pltpu.VMEM((PAIRS, SPACE, ROWS, HD), bf16),
            pltpu.VMEM((PAIRS, 3 * SPACE, ROWS, HD), bf16),
            pltpu.VMEM((PAIRS, 3 * SPACE, ROWS, 2 * HD), bf16),
            pltpu.VMEM((2 * SPACE, PAIRS, ROWS, HD), bf16),
            pltpu.SemaphoreType.DMA((PAIRS, 3)),
            pltpu.SemaphoreType.DMA((PAIRS,)),
        ],
        compiler_params=params(60),
        name="attend",
    )(window, span_slot, counts, came, *wide)
    attended = attended.reshape(2 * SPACE, PAIRS * ROWS, HD)
    attended = lax.all_to_all(
        attended, ("space", "head"), split_axis=0, concat_axis=0, tiled=True
    )

    tile = 512
    tiles = columns // tile
    mixed = pl.pallas_call(
        project,
        out_shape=shape((SPANS * ROWS, columns), bf16),
        in_specs=[HBM] * (2 + GROUPS),
        out_specs=HBM,
        scratch_shapes=[
            pltpu.VMEM((2, SPANS * ROWS, depth), bf16),
            pltpu.VMEM((tiles, depth, tile), bf16),
            pltpu.VMEM((tiles, depth, tile), bf16),
            pltpu.VMEM((tiles, SPANS * ROWS, tile), bf16),
            pltpu.SemaphoreType.DMA((2,)),
            pltpu.SemaphoreType.DMA((tiles, 2)),
            pltpu.SemaphoreType.DMA((tiles,)),
        ],
        compiler_params=params(52),
        name="project",
    )(attended, out_weight, *lent)
    return mixed.reshape(SPANS, ROWS, columns)


def solution(mesh):
    in_specs = (
        P("cache", "space", "head"),
        P("cache", "space", "head"),
        P("cache", "space", "head"),
        P("cache", "space", "head"),
        P("cache", "space", "head"),
        P(),
        P(),
        P(),
        P("head", None),
    )
    out_specs = P("cache", "space", "head")
    return jax.shard_map(
        on_device, mesh=mesh, in_specs=in_specs, out_specs=out_specs, check_vma=False
    )
```

```python
import math

import jax
import jax.numpy as jnp
from jax import lax
from jax.experimental import pallas as pl
from jax.experimental.pallas import tpu as pltpu
from jax.sharding import PartitionSpec as P

HD = 128
WIN = 2
SPANS = 4
GROUPS = 8
SPACE = 8
ROWS = 80
SPAN = SPACE * ROWS
HEADS = 10
WIDE = SPACE * HD
PAIRS = 5
LENT = (0, 1, 3, 4)
EARLY = 2
UNITS = 3 * PAIRS + 2 * WIN - EARLY
BLOCKS = 4
AHEAD = 2
STEPS = ((0, 0), (2, 0), (2, 1), (1, 0), (3, 0), (1, 1), (3, 1), (0, 1))
VMEM = pl.BlockSpec(memory_space=pltpu.VMEM)
HBM = pl.BlockSpec(memory_space=pltpu.HBM)
SMEM = pl.BlockSpec(memory_space=pltpu.SMEM)
MIB = 1 << 20


def params(mib):
    return pltpu.CompilerParams(vmem_limit_bytes=mib * MIB)


def goes_to(me, step):
    ring, cross = STEPS[step]
    return ((((me >> 1) + ring) & 3) << 1) | ((me & 1) ^ cross)


def came_from(me, step):
    ring, cross = STEPS[step]
    return ((((me >> 1) - ring) & 3) << 1) | ((me & 1) ^ cross)


def shift(x, axis, step):
    return lax.ppermute(x, axis, [(i, goes_to(i, step)) for i in range(8)])


def wait_for(ref, sem):
    pltpu.make_async_copy(ref, ref, sem).wait()


def picked(window, span_slot, block, group):
    place = jnp.int32(0)
    for span in range(SPANS):
        for w in range(WIN):
            slot = span_slot[window[w, block * SPANS + span]]
            place = jnp.where((slot >> 1) == group, slot & 1, place)
    return place


def pack_slots(window, span_slot, cache_keys, cache_values, queries, out_weight, by_head, *refs):
    rest, lent = refs[:GROUPS], refs[GROUPS : GROUPS + 2]
    held, queries_held, lent_held, held_sems, sems = refs[GROUPS + 2 :]
    me = lax.axis_index("cache")
    rows, columns = lent[0].shape
    column = pl.multiple_of((1 - lax.axis_index("head")) * columns, HD)
    loads = [
        pltpu.make_async_copy(source, held.at[kv], held_sems.at[kv])
        for kv, source in enumerate((cache_keys, cache_values))
    ]
    source = queries.at[pl.ds(0, EARLY), :, pl.ds(0, WIDE)]
    loads.append(pltpu.make_async_copy(source, queries_held, held_sems.at[2]))
    for part in range(2):
        row = pl.multiple_of((2 * me + part) * rows, 16)
        source = out_weight.at[pl.ds(row, rows), pl.ds(column, columns)]
        loads.append(pltpu.make_async_copy(source, lent_held.at[part], held_sems.at[3 + part]))
    for load in loads:
        load.start()
    for load in loads[:2]:
        load.wait()
    for head in range(SPACE):
        lanes = pl.ds(head * HD, HD)
        for kv in range(2):
            target = by_head.at[head, pl.ds(2 * kv, 2)]
            pltpu.make_async_copy(held.at[kv, :, :, lanes], target, sems.at[0]).start()
    for step in range(GROUPS):
        slot = picked(window, span_slot, goes_to(me, step), me)
        source = held.at[:, slot, :, pl.ds(WIDE, 2 * HD)]
        pltpu.make_async_copy(source, rest[step], sems.at[1 + step]).start()
    loads[2].wait()
    for head in range(SPACE):
        source = queries_held.at[:, :, pl.ds(head * HD, HD)]
        target = by_head.at[head, pl.ds(4, EARLY)]
        pltpu.make_async_copy(source, target, sems.at[0]).start()
    for part in range(2):
        loads[3 + part].wait()
        pltpu.make_async_copy(lent_held.at[part], lent[part], sems.at[1 + GROUPS + part]).start()
    for place, target in enumerate((by_head, *rest, *lent)):
        wait_for(target, sems.at[place])


def unit_of(kind, pair):
    return kind * PAIRS + pair - EARLY


def pack_pairs(queries, keys, values, sent, held, held_sems, sems):
    loads = [
        pltpu.make_async_copy(source, held.at[kind], held_sems.at[kind])
        for kind, source in enumerate((queries, keys, values))
    ]
    for load in loads:
        load.start()
    for kind in range(3):
        first = EARLY if kind == 0 else 0
        loads[kind].wait()
        for to in range(SPACE):
            wide, last = pl.ds(to * HD, HD), pl.ds(WIDE + to % 2 * HD, HD)
            if first < SPANS:
                pltpu.make_async_copy(
                    held.at[kind, pl.ds(first, SPANS - first), :, wide],
                    sent.at[to, pl.ds(unit_of(kind, first), SPANS - first)],
                    sems.at[kind],
                ).start()
            pltpu.make_async_copy(
                held.at[kind, to // 2, :, last], sent.at[to, unit_of(kind, SPANS)], sems.at[kind]
            ).start()
    for kind in range(3):
        first = EARLY if kind == 0 else 0
        wait_for(sent.at[:, pl.ds(unit_of(kind, first), PAIRS - first)], sems.at[kind])


def pack_cached(window, span_slot, by_head, *refs):
    rest, sent, wide = refs[:GROUPS], refs[GROUPS + 1], refs[GROUPS + 2 : 2 * GROUPS + 2]
    held, heads, held_sems, wide_sems, sent_sem = refs[2 * GROUPS + 2 :]
    group = lax.axis_index("cache")
    loads = [pltpu.make_async_copy(by_head.at[:, pl.ds(0, 4)], heads, held_sems.at[GROUPS])]
    for step in range(GROUPS):
        target = held.at[came_from(group, step)]
        loads.append(pltpu.make_async_copy(rest[step], target, held_sems.at[step]))
    for load in loads:
        load.start()
    loads[0].wait()
    for step in range(GROUPS):
        slot = picked(window, span_slot, goes_to(group, step), group)
        for kv in range(2):
            source = heads.at[:, 2 * kv + slot]
            pltpu.make_async_copy(source, wide[step].at[kv], wide_sems.at[step]).start()
    for load in loads[1:]:
        load.wait()
    for to in range(SPACE):
        for w in range(WIN):
            owner = span_slot[window[w, group * SPANS + to // 2]] >> 1
            pltpu.make_async_copy(
                held.at[owner, :, :, pl.ds(to % 2 * HD, HD)],
                sent.at[to, pl.ds(unit_of(3, 2 * w), 2)],
                sent_sem.at[0],
            ).start()
    for step in range(GROUPS):
        wait_for(wide[step], wide_sems.at[step])
    wait_for(sent.at[:, pl.ds(unit_of(3, 0), 2 * WIN)], sent_sem.at[0])


def attend(window, span_slot, counts, *refs):
    early, came, wide = refs[0], refs[1], refs[2 : 2 + GROUPS]
    out, q_all, k_all, v_all, sent, ready, left = refs[2 + GROUPS :]
    group = lax.axis_index("cache")
    me = lax.axis_index("space")
    factor = math.log2(math.e) / math.sqrt(HD)

    def fetch(pair, kind, source, target):
        pltpu.make_async_copy(source, target, ready.at[pair, kind]).start()

    def share(pair, kind, segment):
        if kind == 0:
            return q_all.at[pair]
        chunks = pl.ds(segment * SPACE, SPACE)
        if kind == 1:
            return k_all.at[pair, chunks]
        return v_all.at[pair, chunks, :, pl.ds(0, HD)]

    def fetch_pair(pair):
        for kind in range(3):
            before = kind == 0 and pair < EARLY
            source = early.at[:, 4 + pair] if before else came.at[:, unit_of(kind, pair)]
            fetch(pair, kind, source, share(pair, kind, 0))

    def fetch_wide(step, place):
        pair, segment = place >> 1, 1 + (place & 1)
        for kv in range(2):
            fetch(pair, 1 + kv, wide[step].at[kv], share(pair, 1 + kv, segment))

    fetch_pair(0)
    places = []
    for step in range(GROUPS):
        owner = came_from(group, step)
        place = jnp.int32(0)
        for entry in range(SPANS * WIN):
            slot = span_slot[window[entry % 2, group * SPANS + entry // 2]]
            place = jnp.where((slot >> 1) == owner, entry, place)
        places.append(place)
        pl.when(place < WIN)(lambda: fetch_wide(step, place))
    v_all[:, :, :, HD:] = jnp.ones((PAIRS, 3 * SPACE, ROWS, HD), jnp.bfloat16)

    def prepare(pair):
        for kind in range(3):
            wait_for(q_all.at[pair] if kind == 0 else k_all.at[pair], ready.at[pair, kind])
        span = me >> 1 if pair == SPANS else pair
        for w in range(WIN):
            limit = counts[window[w, group * SPANS + span]]
            first = (1 + w) * SPACE
            half = slice(first + SPACE // 2, first + SPACE)
            extent = (SPACE // 2, ROWS, HD)
            spots = SPAN // 2 + lax.broadcasted_iota(jnp.int32, extent, 1)
            valid = spots + ROWS * lax.broadcasted_iota(jnp.int32, extent, 0) < limit
            key = k_all[pair, first, 0:1].astype(jnp.float32)
            key = jnp.broadcast_to(key[None], extent)
            held = k_all[pair, half].astype(jnp.float32)
            k_all[pair, half] = jnp.where(valid, held, key).astype(jnp.bfloat16)
            held = v_all[pair, half, :, 0:HD].astype(jnp.float32)
            v_all[pair, half, :, 0:HD] = jnp.where(valid, held, 0.0).astype(jnp.bfloat16)
            v_all[pair, half, :, HD:] = jnp.where(valid, 1.0, 0.0).astype(jnp.bfloat16)

    block = SPACE // BLOCKS

    def score(pair, part):
        query = q_all[pair, part * block : (part + 1) * block].reshape(block * ROWS, HD)
        key = k_all[pair].reshape(3 * SPAN, HD)
        return lax.dot_general(
            query, key, (((1,), (1,)), ((), ())), preferred_element_type=jnp.float32
        )

    def finish(pair, part, scores):
        top = jnp.max(scores, axis=1, keepdims=True)
        weights = jnp.exp2((scores - top) * factor).astype(jnp.bfloat16)
        value = v_all[pair].reshape(3 * SPAN, 2 * HD)
        both = jnp.dot(weights, value, preferred_element_type=jnp.float32)
        done = (both[:, 0:HD] / both[:, HD:]).astype(jnp.bfloat16).reshape(block, ROWS, HD)
        for place in range(block):
            for half in range(2):
                sent[2 * (part * block + place) + half, pair] = done[place]

    steps = [(pair, part) for pair in range(PAIRS) for part in range(BLOCKS)]
    prepare(0)
    for step, place in enumerate(places):
        pl.when(place >= WIN)(lambda: fetch_wide(step, place))
    for pair in range(1, PAIRS):
        fetch_pair(pair)
    for w in range(WIN):
        for kv in range(2):
            source = came.at[:, unit_of(3, 2 * w + kv)]
            fetch(SPANS, 1 + kv, source, share(SPANS, 1 + kv, 1 + w))
    scores = score(0, 0)
    for now, later in zip(steps, steps[1:] + [None]):
        held = scores
        if later is not None:
            if later[1] == 0:
                prepare(later[0])
            scores = score(*later)
        finish(*now, held)
        if now[1] == BLOCKS - 1:
            pair = now[0]
            pltpu.make_async_copy(sent.at[:, pair], out.at[:, pair], left.at[pair]).start()

    for pair in range(PAIRS):
        pltpu.make_async_copy(sent.at[:, pair], out.at[:, pair], left.at[pair]).wait()


def project(came, own_weight, *refs):
    lent, out, features, own, other, mixed, came_sems, weight_sems, out_sems = (
        refs[:GROUPS],
        *refs[GROUPS:],
    )
    group = lax.axis_index("cache")
    half = lax.axis_index("head")
    columns = out.shape[1]
    rows = lent[0].shape[0]
    tiles = weight_sems.shape[0]
    tile = columns // tiles
    for part in range(2):
        source = half if part == 0 else 1 - half
        for space in range(SPACE):
            pltpu.make_async_copy(
                came.at[2 * space + source, pl.ds(0, SPANS * ROWS)],
                features.at[part, :, pl.ds(space * HD, HD)],
                came_sems.at[part],
            ).start()
            pltpu.make_async_copy(
                came.at[2 * space + source, pl.ds(SPANS * ROWS, ROWS)],
                features.at[
                    part, pl.ds(space // 2 * ROWS, ROWS), pl.ds(WIDE + space % 2 * HD, HD)
                ],
                came_sems.at[part],
            ).start()

    def fetch(step):
        here = pl.ds(step * tile, tile)
        start = pl.multiple_of(half * columns + step * tile, 128)
        pltpu.make_async_copy(
            own_weight.at[:, pl.ds(start, tile)], own.at[step], weight_sems.at[step, 0]
        ).start()
        for place, chunk in enumerate(lent):
            holder = group ^ (place // 4)
            start = pl.multiple_of(came_from(holder, LENT[place % 4]) * rows, 16)
            pltpu.make_async_copy(
                chunk.at[:, here], other.at[step, pl.ds(start, rows)], weight_sems.at[step, 1]
            ).start()

    for step in range(AHEAD):
        fetch(step)
    for part in range(2):
        wait_for(features.at[part], came_sems.at[part])
    for step in range(tiles):
        here = pl.ds(step * tile, tile)
        wait_for(own.at[step], weight_sems.at[step, 0])
        wait_for(other.at[step], weight_sems.at[step, 1])
        if step + AHEAD < tiles:
            fetch(step + AHEAD)
        total = jnp.dot(features[0], own[step], preferred_element_type=jnp.float32)
        total += jnp.dot(features[1], other[step], preferred_element_type=jnp.float32)
        mixed[step] = total.astype(jnp.bfloat16)
        pltpu.make_async_copy(mixed.at[step], out.at[:, here], out_sems.at[step]).start()
    for step in range(tiles):
        here = pl.ds(step * tile, tile)
        pltpu.make_async_copy(mixed.at[step], out.at[:, here], out_sems.at[step]).wait()


def on_device(
    queries, keys, values, cache_keys, cache_values, window, span_slot, counts, out_weight
):
    bf16 = jnp.bfloat16
    shape = jax.ShapeDtypeStruct
    depth, width = out_weight.shape
    columns = width // 2

    rows = depth // GROUPS // 2
    window = window.T

    by_head, *sent = pl.pallas_call(
        pack_slots,
        out_shape=[shape((SPACE, 4 + EARLY, ROWS, HD), bf16)]
        + [shape((2, ROWS, 2 * HD), bf16)] * GROUPS
        + [shape((rows, columns), bf16)] * 2,
        in_specs=[SMEM] * 2 + [HBM] * 4,
        out_specs=[HBM] * (3 + GROUPS),
        scratch_shapes=[
            pltpu.VMEM((2, 2, ROWS, HEADS * HD), bf16),
            pltpu.VMEM((EARLY, ROWS, WIDE), bf16),
            pltpu.VMEM((2, rows, columns), bf16),
            pltpu.SemaphoreType.DMA((5,)),
            pltpu.SemaphoreType.DMA((3 + GROUPS,)),
        ],
        compiler_params=params(60),
        name="pack_slots",
    )(window, span_slot, cache_keys, cache_values, queries, out_weight)
    by_head, *sent, queries = lax.optimization_barrier((by_head, *sent, queries))
    rest, lent = sent[:GROUPS], sent[GROUPS:]
    by_head = lax.all_to_all(
        by_head.reshape(SPACE, -1, HD), "space", split_axis=0, concat_axis=0, tiled=True
    ).reshape(by_head.shape)
    rest = [rest[0]] + [shift(rest[step], "cache", step) for step in range(1, GROUPS)]
    lent = [
        lax.ppermute(lent[0], "head", [(0, 1), (1, 0)]),
        lax.ppermute(lent[1], ("space", "head"), [(i, i ^ 3) for i in range(2 * SPACE)]),
    ]
    pairs = pl.pallas_call(
        pack_pairs,
        out_shape=shape((SPACE, UNITS, ROWS, HD), bf16),
        in_specs=[HBM] * 3,
        out_specs=HBM,
        scratch_shapes=[
            pltpu.VMEM((3, SPANS, ROWS, HEADS * HD), bf16),
            pltpu.SemaphoreType.DMA((3,)),
            pltpu.SemaphoreType.DMA((3,)),
        ],
        compiler_params=params(60),
        name="pack_pairs",
    )(queries, keys, values)
    by_head, *rest = lax.optimization_barrier((by_head, *rest))
    pairs, *wide = pl.pallas_call(
        pack_cached,
        out_shape=[shape(pairs.shape, bf16)] + [shape((2, SPACE, ROWS, HD), bf16)] * GROUPS,
        in_specs=[SMEM] * 2 + [HBM] * (2 + GROUPS),
        out_specs=[HBM] * (1 + GROUPS),
        input_output_aliases={3 + GROUPS: 0},
        scratch_shapes=[
            pltpu.VMEM((GROUPS, 2, ROWS, 2 * HD), bf16),
            pltpu.VMEM((SPACE, 4, ROWS, HD), bf16),
            pltpu.SemaphoreType.DMA((GROUPS + 1,)),
            pltpu.SemaphoreType.DMA((GROUPS,)),
            pltpu.SemaphoreType.DMA((1,)),
        ],
        compiler_params=params(60),
        name="pack_cached",
    )(window, span_slot, by_head, *rest, pairs)
    pairs, *lent = lax.optimization_barrier((pairs, *lent))
    came = lax.all_to_all(
        pairs.reshape(SPACE, UNITS * ROWS, HD), "space", split_axis=0, concat_axis=0, tiled=True
    ).reshape(pairs.shape)
    wide = [wide[0]] + [shift(wide[step], "cache", step) for step in range(1, GROUPS)]
    lent = jnp.concatenate(lent, 0)
    lent, *wide = lax.optimization_barrier((lent, *wide))
    lent = [lent] + [shift(lent, "cache", step) for step in LENT[1:]]
    lent += [lax.ppermute(chunk, "cache", [(i, i ^ 1) for i in range(8)]) for chunk in lent]

    attended = pl.pallas_call(
        attend,
        out_shape=shape((2 * SPACE, PAIRS, ROWS, HD), bf16),
        in_specs=[SMEM] * 3 + [HBM] * (2 + GROUPS),
        out_specs=HBM,
        scratch_shapes=[
            pltpu.VMEM((PAIRS, SPACE, ROWS, HD), bf16),
            pltpu.VMEM((PAIRS, 3 * SPACE, ROWS, HD), bf16),
            pltpu.VMEM((PAIRS, 3 * SPACE, ROWS, 2 * HD), bf16),
            pltpu.VMEM((2 * SPACE, PAIRS, ROWS, HD), bf16),
            pltpu.SemaphoreType.DMA((PAIRS, 3)),
            pltpu.SemaphoreType.DMA((PAIRS,)),
        ],
        compiler_params=params(60),
        name="attend",
    )(window, span_slot, counts, by_head, came, *wide)
    attended = attended.reshape(2 * SPACE, PAIRS * ROWS, HD)
    attended = lax.all_to_all(
        attended, ("space", "head"), split_axis=0, concat_axis=0, tiled=True
    )

    tile = 512
    tiles = columns // tile
    mixed = pl.pallas_call(
        project,
        out_shape=shape((SPANS * ROWS, columns), bf16),
        in_specs=[HBM] * (2 + GROUPS),
        out_specs=HBM,
        scratch_shapes=[
            pltpu.VMEM((2, SPANS * ROWS, depth), bf16),
            pltpu.VMEM((tiles, depth, tile), bf16),
            pltpu.VMEM((tiles, depth, tile), bf16),
            pltpu.VMEM((tiles, SPANS * ROWS, tile), bf16),
            pltpu.SemaphoreType.DMA((2,)),
            pltpu.SemaphoreType.DMA((tiles, 2)),
            pltpu.SemaphoreType.DMA((tiles,)),
        ],
        compiler_params=params(52),
        name="project",
    )(attended, out_weight, *lent)
    return mixed.reshape(SPANS, ROWS, columns)


def solution(mesh):
    in_specs = (
        P("cache", "space", "head"),
        P("cache", "space", "head"),
        P("cache", "space", "head"),
        P("cache", "space", "head"),
        P("cache", "space", "head"),
        P(),
        P(),
        P(),
        P("head", None),
    )
    out_specs = P("cache", "space", "head")
    return jax.shard_map(
        on_device, mesh=mesh, in_specs=in_specs, out_specs=out_specs, check_vma=False
    )
```

```python
import math

import jax
import jax.numpy as jnp
from jax import lax
from jax.experimental import pallas as pl
from jax.experimental.pallas import tpu as pltpu
from jax.sharding import PartitionSpec as P

HD = 128
WIN = 2
SPANS = 4
GROUPS = 8
SPACE = 8
ROWS = 80
SPAN = SPACE * ROWS
HEADS = 10
WIDE = SPACE * HD
PAIRS = 5
LENT = (0, 1, 3, 4)
EARLY = 2
UNITS = 3 * PAIRS + 2 * WIN - EARLY
BLOCKS = 4
AHEAD = 2
STEPS = ((0, 0), (2, 0), (2, 1), (1, 0), (3, 0), (1, 1), (3, 1), (0, 1))
VMEM = pl.BlockSpec(memory_space=pltpu.VMEM)
HBM = pl.BlockSpec(memory_space=pltpu.HBM)
SMEM = pl.BlockSpec(memory_space=pltpu.SMEM)
MIB = 1 << 20


def params(mib):
    return pltpu.CompilerParams(vmem_limit_bytes=mib * MIB)


def goes_to(me, step):
    ring, cross = STEPS[step]
    return ((((me >> 1) + ring) & 3) << 1) | ((me & 1) ^ cross)


def came_from(me, step):
    ring, cross = STEPS[step]
    return ((((me >> 1) - ring) & 3) << 1) | ((me & 1) ^ cross)


def shift(x, axis, step):
    return lax.ppermute(x, axis, [(i, goes_to(i, step)) for i in range(8)])


def wait_for(ref, sem):
    pltpu.make_async_copy(ref, ref, sem).wait()


def picked(window, span_slot, block, group):
    place = jnp.int32(0)
    for span in range(SPANS):
        for w in range(WIN):
            slot = span_slot[window[w, block * SPANS + span]]
            place = jnp.where((slot >> 1) == group, slot & 1, place)
    return place


def owners_of(window, span_slot, group):
    return [
        span_slot[window[w, group * SPANS + span]] >> 1 for span in range(SPANS) for w in range(WIN)
    ]


def pack_slots(window, span_slot, cache_keys, cache_values, queries, out_weight, by_head, *refs):
    rest, lent = refs[:GROUPS], refs[GROUPS : GROUPS + 2]
    held, queries_held, lent_held, held_sems, sems = refs[GROUPS + 2 :]
    me = lax.axis_index("cache")
    rows, columns = lent[0].shape
    column = pl.multiple_of((1 - lax.axis_index("head")) * columns, HD)
    loads = [
        pltpu.make_async_copy(source, held.at[kv], held_sems.at[kv])
        for kv, source in enumerate((cache_keys, cache_values))
    ]
    source = queries.at[pl.ds(0, EARLY), :, pl.ds(0, WIDE)]
    loads.append(pltpu.make_async_copy(source, queries_held, held_sems.at[2]))
    for part in range(2):
        row = pl.multiple_of((2 * me + part) * rows, 16)
        source = out_weight.at[pl.ds(row, rows), pl.ds(column, columns)]
        loads.append(pltpu.make_async_copy(source, lent_held.at[part], held_sems.at[3 + part]))
    for load in loads:
        load.start()
    slots = [picked(window, span_slot, goes_to(me, step), me) for step in range(GROUPS)]
    for kv in range(2):
        loads[kv].wait()
        for head in range(SPACE):
            source = held.at[kv, :, :, pl.ds(head * HD, HD)]
            target = by_head.at[head, pl.ds(2 * kv, 2)]
            pltpu.make_async_copy(source, target, sems.at[0]).start()
    for step, slot in enumerate(slots):
        source = held.at[:, slot, :, pl.ds(WIDE, 2 * HD)]
        pltpu.make_async_copy(source, rest[step], sems.at[1 + step]).start()
    loads[2].wait()
    for head in range(SPACE):
        source = queries_held.at[:, :, pl.ds(head * HD, HD)]
        target = by_head.at[head, pl.ds(4, EARLY)]
        pltpu.make_async_copy(source, target, sems.at[0]).start()
    for part in range(2):
        loads[3 + part].wait()
        pltpu.make_async_copy(lent_held.at[part], lent[part], sems.at[1 + GROUPS + part]).start()
    for place, target in enumerate((by_head, *rest, *lent)):
        wait_for(target, sems.at[place])


def unit_of(kind, pair):
    return kind * PAIRS + pair - EARLY


def pack_pairs(queries, keys, values, sent, held, held_sems, sems):
    loads = [
        pltpu.make_async_copy(source, held.at[kind], held_sems.at[kind])
        for kind, source in enumerate((queries, keys, values))
    ]
    for load in loads:
        load.start()
    for kind in range(3):
        first = EARLY if kind == 0 else 0
        loads[kind].wait()
        for to in range(SPACE):
            wide, last = pl.ds(to * HD, HD), pl.ds(WIDE + to % 2 * HD, HD)
            if first < SPANS:
                pltpu.make_async_copy(
                    held.at[kind, pl.ds(first, SPANS - first), :, wide],
                    sent.at[to, pl.ds(unit_of(kind, first), SPANS - first)],
                    sems.at[kind],
                ).start()
            pltpu.make_async_copy(
                held.at[kind, to // 2, :, last], sent.at[to, unit_of(kind, SPANS)], sems.at[kind]
            ).start()
    for kind in range(3):
        first = EARLY if kind == 0 else 0
        wait_for(sent.at[:, pl.ds(unit_of(kind, first), PAIRS - first)], sems.at[kind])


def pack_cached(window, span_slot, by_head, *refs):
    rest, sent, wide = refs[:GROUPS], refs[GROUPS + 1], refs[GROUPS + 2 : 2 * GROUPS + 2]
    held, heads, held_sems, wide_sems, sent_sem = refs[2 * GROUPS + 2 :]
    group = lax.axis_index("cache")
    loads = [pltpu.make_async_copy(by_head.at[:, pl.ds(0, 4)], heads, held_sems.at[GROUPS])]
    for step in range(GROUPS):
        target = held.at[came_from(group, step)]
        loads.append(pltpu.make_async_copy(rest[step], target, held_sems.at[step]))
    for load in loads:
        load.start()
    slots = [picked(window, span_slot, goes_to(group, step), group) for step in range(GROUPS)]
    owners = owners_of(window, span_slot, group)
    loads[0].wait()
    for step, slot in enumerate(slots):
        for kv in range(2):
            source = heads.at[:, 2 * kv + slot]
            pltpu.make_async_copy(source, wide[step].at[kv], wide_sems.at[step]).start()
    for load in loads[1:]:
        load.wait()
    for to in range(SPACE):
        for w in range(WIN):
            owner = owners[to // 2 * WIN + w]
            pltpu.make_async_copy(
                held.at[owner, :, :, pl.ds(to % 2 * HD, HD)],
                sent.at[to, pl.ds(unit_of(3, 2 * w), 2)],
                sent_sem.at[0],
            ).start()
    for step in range(GROUPS):
        wait_for(wide[step], wide_sems.at[step])
    wait_for(sent.at[:, pl.ds(unit_of(3, 0), 2 * WIN)], sent_sem.at[0])


def attend(window, span_slot, counts, *refs):
    early, came, wide = refs[0], refs[1], refs[2 : 2 + GROUPS]
    out, q_all, k_all, v_all, sent, ready, left = refs[2 + GROUPS :]
    group = lax.axis_index("cache")
    me = lax.axis_index("space")
    factor = math.log2(math.e) / math.sqrt(HD)

    def fetch(pair, kind, source, target):
        pltpu.make_async_copy(source, target, ready.at[pair, kind]).start()

    def share(pair, kind, segment):
        if kind == 0:
            return q_all.at[pair]
        chunks = pl.ds(segment * SPACE, SPACE)
        if kind == 1:
            return k_all.at[pair, chunks]
        return v_all.at[pair, chunks, :, pl.ds(0, HD)]

    def fetch_pair(pair):
        for kind in range(3):
            before = kind == 0 and pair < EARLY
            source = early.at[:, 4 + pair] if before else came.at[:, unit_of(kind, pair)]
            fetch(pair, kind, source, share(pair, kind, 0))

    def fetch_wide(step, place):
        pair, segment = place >> 1, 1 + (place & 1)
        for kv in range(2):
            fetch(pair, 1 + kv, wide[step].at[kv], share(pair, 1 + kv, segment))

    fetch_pair(0)
    owners = owners_of(window, span_slot, group)
    places = []
    for step in range(GROUPS):
        source = came_from(group, step)
        place = jnp.int32(0)
        for entry, owner in enumerate(owners):
            place = jnp.where(owner == source, entry, place)
        places.append(place)
        pl.when(place < WIN)(lambda: fetch_wide(step, place))
    v_all[:, :, :, HD:] = jnp.ones((PAIRS, 3 * SPACE, ROWS, HD), jnp.bfloat16)

    def prepare(pair):
        for kind in range(3):
            wait_for(q_all.at[pair] if kind == 0 else k_all.at[pair], ready.at[pair, kind])
        span = me >> 1 if pair == SPANS else pair
        for w in range(WIN):
            limit = counts[window[w, group * SPANS + span]]
            first = (1 + w) * SPACE
            half = slice(first + SPACE // 2, first + SPACE)
            extent = (SPACE // 2, ROWS, HD)
            spots = SPAN // 2 + lax.broadcasted_iota(jnp.int32, extent, 1)
            valid = spots + ROWS * lax.broadcasted_iota(jnp.int32, extent, 0) < limit
            key = k_all[pair, first, 0:1].astype(jnp.float32)
            key = jnp.broadcast_to(key[None], extent)
            held = k_all[pair, half].astype(jnp.float32)
            k_all[pair, half] = jnp.where(valid, held, key).astype(jnp.bfloat16)
            held = v_all[pair, half, :, 0:HD].astype(jnp.float32)
            v_all[pair, half, :, 0:HD] = jnp.where(valid, held, 0.0).astype(jnp.bfloat16)
            v_all[pair, half, :, HD:] = jnp.where(valid, 1.0, 0.0).astype(jnp.bfloat16)

    block = SPACE // BLOCKS

    def score(pair, part):
        query = q_all[pair, part * block : (part + 1) * block].reshape(block * ROWS, HD)
        key = k_all[pair].reshape(3 * SPAN, HD)
        return lax.dot_general(
            query, key, (((1,), (1,)), ((), ())), preferred_element_type=jnp.float32
        )

    def finish(pair, part, scores):
        top = jnp.max(scores, axis=1, keepdims=True)
        weights = jnp.exp2((scores - top) * factor).astype(jnp.bfloat16)
        value = v_all[pair].reshape(3 * SPAN, 2 * HD)
        both = jnp.dot(weights, value, preferred_element_type=jnp.float32)
        done = (both[:, 0:HD] / both[:, HD:]).astype(jnp.bfloat16).reshape(block, ROWS, HD)
        for place in range(block):
            for half in range(2):
                sent[2 * (part * block + place) + half, pair] = done[place]

    steps = [(pair, part) for pair in range(PAIRS) for part in range(BLOCKS)]
    prepare(0)
    for step, place in enumerate(places):
        pl.when(place >= WIN)(lambda: fetch_wide(step, place))
    for pair in range(1, PAIRS):
        fetch_pair(pair)
    for w in range(WIN):
        for kv in range(2):
            source = came.at[:, unit_of(3, 2 * w + kv)]
            fetch(SPANS, 1 + kv, source, share(SPANS, 1 + kv, 1 + w))
    scores = score(0, 0)
    for now, later in zip(steps, steps[1:] + [None]):
        held = scores
        if later is not None:
            if later[1] == 0:
                prepare(later[0])
            scores = score(*later)
        finish(*now, held)
        if now[1] == BLOCKS - 1:
            pair = now[0]
            pltpu.make_async_copy(sent.at[:, pair], out.at[:, pair], left.at[pair]).start()

    for pair in range(PAIRS):
        pltpu.make_async_copy(sent.at[:, pair], out.at[:, pair], left.at[pair]).wait()


def project(came, own_weight, *refs):
    lent, out, features, own, other, mixed, came_sems, weight_sems, out_sems = (
        refs[:GROUPS],
        *refs[GROUPS:],
    )
    group = lax.axis_index("cache")
    half = lax.axis_index("head")
    columns = out.shape[1]
    rows = lent[0].shape[0]
    tiles = weight_sems.shape[0]
    tile = columns // tiles
    for part in range(2):
        source = half if part == 0 else 1 - half
        for space in range(SPACE):
            pltpu.make_async_copy(
                came.at[2 * space + source, pl.ds(0, SPANS * ROWS)],
                features.at[part, :, pl.ds(space * HD, HD)],
                came_sems.at[part],
            ).start()
            pltpu.make_async_copy(
                came.at[2 * space + source, pl.ds(SPANS * ROWS, ROWS)],
                features.at[
                    part, pl.ds(space // 2 * ROWS, ROWS), pl.ds(WIDE + space % 2 * HD, HD)
                ],
                came_sems.at[part],
            ).start()

    def fetch(step):
        here = pl.ds(step * tile, tile)
        start = pl.multiple_of(half * columns + step * tile, 128)
        pltpu.make_async_copy(
            own_weight.at[:, pl.ds(start, tile)], own.at[step], weight_sems.at[step, 0]
        ).start()
        for place, chunk in enumerate(lent):
            holder = group ^ (place // 4)
            start = pl.multiple_of(came_from(holder, LENT[place % 4]) * rows, 16)
            pltpu.make_async_copy(
                chunk.at[:, here], other.at[step, pl.ds(start, rows)], weight_sems.at[step, 1]
            ).start()

    for step in range(AHEAD):
        fetch(step)
    for part in range(2):
        wait_for(features.at[part], came_sems.at[part])
    for step in range(tiles):
        here = pl.ds(step * tile, tile)
        wait_for(own.at[step], weight_sems.at[step, 0])
        wait_for(other.at[step], weight_sems.at[step, 1])
        if step + AHEAD < tiles:
            fetch(step + AHEAD)
        total = jnp.dot(features[0], own[step], preferred_element_type=jnp.float32)
        total += jnp.dot(features[1], other[step], preferred_element_type=jnp.float32)
        mixed[step] = total.astype(jnp.bfloat16)
        pltpu.make_async_copy(mixed.at[step], out.at[:, here], out_sems.at[step]).start()
    for step in range(tiles):
        here = pl.ds(step * tile, tile)
        pltpu.make_async_copy(mixed.at[step], out.at[:, here], out_sems.at[step]).wait()


def on_device(
    queries, keys, values, cache_keys, cache_values, window, span_slot, counts, out_weight
):
    bf16 = jnp.bfloat16
    shape = jax.ShapeDtypeStruct
    depth, width = out_weight.shape
    columns = width // 2

    rows = depth // GROUPS // 2
    window = window.T

    by_head, *sent = pl.pallas_call(
        pack_slots,
        out_shape=[shape((SPACE, 4 + EARLY, ROWS, HD), bf16)]
        + [shape((2, ROWS, 2 * HD), bf16)] * GROUPS
        + [shape((rows, columns), bf16)] * 2,
        in_specs=[SMEM] * 2 + [HBM] * 4,
        out_specs=[HBM] * (3 + GROUPS),
        scratch_shapes=[
            pltpu.VMEM((2, 2, ROWS, HEADS * HD), bf16),
            pltpu.VMEM((EARLY, ROWS, WIDE), bf16),
            pltpu.VMEM((2, rows, columns), bf16),
            pltpu.SemaphoreType.DMA((5,)),
            pltpu.SemaphoreType.DMA((3 + GROUPS,)),
        ],
        compiler_params=params(60),
        name="pack_slots",
    )(window, span_slot, cache_keys, cache_values, queries, out_weight)
    by_head, *sent, queries = lax.optimization_barrier((by_head, *sent, queries))
    rest, lent = sent[:GROUPS], sent[GROUPS:]
    by_head = lax.all_to_all(
        by_head.reshape(SPACE, -1, HD), "space", split_axis=0, concat_axis=0, tiled=True
    ).reshape(by_head.shape)
    rest = [rest[0]] + [shift(rest[step], "cache", step) for step in range(1, GROUPS)]
    lent = [
        lax.ppermute(lent[0], "head", [(0, 1), (1, 0)]),
        lax.ppermute(lent[1], ("space", "head"), [(i, i ^ 3) for i in range(2 * SPACE)]),
    ]
    pairs = pl.pallas_call(
        pack_pairs,
        out_shape=shape((SPACE, UNITS, ROWS, HD), bf16),
        in_specs=[HBM] * 3,
        out_specs=HBM,
        scratch_shapes=[
            pltpu.VMEM((3, SPANS, ROWS, HEADS * HD), bf16),
            pltpu.SemaphoreType.DMA((3,)),
            pltpu.SemaphoreType.DMA((3,)),
        ],
        compiler_params=params(60),
        name="pack_pairs",
    )(queries, keys, values)
    by_head, *rest = lax.optimization_barrier((by_head, *rest))
    pairs, *wide = pl.pallas_call(
        pack_cached,
        out_shape=[shape(pairs.shape, bf16)] + [shape((2, SPACE, ROWS, HD), bf16)] * GROUPS,
        in_specs=[SMEM] * 2 + [HBM] * (2 + GROUPS),
        out_specs=[HBM] * (1 + GROUPS),
        input_output_aliases={3 + GROUPS: 0},
        scratch_shapes=[
            pltpu.VMEM((GROUPS, 2, ROWS, 2 * HD), bf16),
            pltpu.VMEM((SPACE, 4, ROWS, HD), bf16),
            pltpu.SemaphoreType.DMA((GROUPS + 1,)),
            pltpu.SemaphoreType.DMA((GROUPS,)),
            pltpu.SemaphoreType.DMA((1,)),
        ],
        compiler_params=params(60),
        name="pack_cached",
    )(window, span_slot, by_head, *rest, pairs)
    pairs, *lent = lax.optimization_barrier((pairs, *lent))
    came = lax.all_to_all(
        pairs.reshape(SPACE, UNITS * ROWS, HD), "space", split_axis=0, concat_axis=0, tiled=True
    ).reshape(pairs.shape)
    wide = [wide[0]] + [shift(wide[step], "cache", step) for step in range(1, GROUPS)]
    lent = jnp.concatenate(lent, 0)
    lent, *wide = lax.optimization_barrier((lent, *wide))
    lent = [lent] + [shift(lent, "cache", step) for step in LENT[1:]]
    lent += [lax.ppermute(chunk, "cache", [(i, i ^ 1) for i in range(8)]) for chunk in lent]

    attended = pl.pallas_call(
        attend,
        out_shape=shape((2 * SPACE, PAIRS, ROWS, HD), bf16),
        in_specs=[SMEM] * 3 + [HBM] * (2 + GROUPS),
        out_specs=HBM,
        scratch_shapes=[
            pltpu.VMEM((PAIRS, SPACE, ROWS, HD), bf16),
            pltpu.VMEM((PAIRS, 3 * SPACE, ROWS, HD), bf16),
            pltpu.VMEM((PAIRS, 3 * SPACE, ROWS, 2 * HD), bf16),
            pltpu.VMEM((2 * SPACE, PAIRS, ROWS, HD), bf16),
            pltpu.SemaphoreType.DMA((PAIRS, 3)),
            pltpu.SemaphoreType.DMA((PAIRS,)),
        ],
        compiler_params=params(60),
        name="attend",
    )(window, span_slot, counts, by_head, came, *wide)
    attended = attended.reshape(2 * SPACE, PAIRS * ROWS, HD)
    attended = lax.all_to_all(
        attended, ("space", "head"), split_axis=0, concat_axis=0, tiled=True
    )

    tile = 512
    tiles = columns // tile
    mixed = pl.pallas_call(
        project,
        out_shape=shape((SPANS * ROWS, columns), bf16),
        in_specs=[HBM] * (2 + GROUPS),
        out_specs=HBM,
        scratch_shapes=[
            pltpu.VMEM((2, SPANS * ROWS, depth), bf16),
            pltpu.VMEM((tiles, depth, tile), bf16),
            pltpu.VMEM((tiles, depth, tile), bf16),
            pltpu.VMEM((tiles, SPANS * ROWS, tile), bf16),
            pltpu.SemaphoreType.DMA((2,)),
            pltpu.SemaphoreType.DMA((tiles, 2)),
            pltpu.SemaphoreType.DMA((tiles,)),
        ],
        compiler_params=params(52),
        name="project",
    )(attended, out_weight, *lent)
    return mixed.reshape(SPANS, ROWS, columns)


def solution(mesh):
    in_specs = (
        P("cache", "space", "head"),
        P("cache", "space", "head"),
        P("cache", "space", "head"),
        P("cache", "space", "head"),
        P("cache", "space", "head"),
        P(),
        P(),
        P(),
        P("head", None),
    )
    out_specs = P("cache", "space", "head")
    return jax.shard_map(
        on_device, mesh=mesh, in_specs=in_specs, out_specs=out_specs, check_vma=False
    )
```

```python
import math

import jax
import jax.numpy as jnp
from jax import lax
from jax.experimental import pallas as pl
from jax.experimental.pallas import tpu as pltpu
from jax.sharding import PartitionSpec as P

HD = 128
WIN = 2
SPANS = 4
GROUPS = 8
SPACE = 8
ROWS = 80
SPAN = SPACE * ROWS
HEADS = 10
WIDE = SPACE * HD
PAIRS = 5
LENT = (0, 1, 3, 4)
EARLY = 2
UNITS = 3 * PAIRS + 2 * WIN - EARLY
BLOCKS = 4
AHEAD = 2
STEPS = ((0, 0), (2, 0), (2, 1), (1, 0), (3, 0), (1, 1), (3, 1), (0, 1))
VMEM = pl.BlockSpec(memory_space=pltpu.VMEM)
HBM = pl.BlockSpec(memory_space=pltpu.HBM)
SMEM = pl.BlockSpec(memory_space=pltpu.SMEM)
MIB = 1 << 20


def params(mib):
    return pltpu.CompilerParams(vmem_limit_bytes=mib * MIB)


def goes_to(me, step):
    ring, cross = STEPS[step]
    return ((((me >> 1) + ring) & 3) << 1) | ((me & 1) ^ cross)


def came_from(me, step):
    ring, cross = STEPS[step]
    return ((((me >> 1) - ring) & 3) << 1) | ((me & 1) ^ cross)


def shift(x, axis, step):
    return lax.ppermute(x, axis, [(i, goes_to(i, step)) for i in range(8)])


def wait_for(ref, sem):
    pltpu.make_async_copy(ref, ref, sem).wait()


def picked(window, span_slot, block, group):
    place = jnp.int32(0)
    for span in range(SPANS):
        for w in range(WIN):
            slot = span_slot[window[w, block * SPANS + span]]
            place = jnp.where((slot >> 1) == group, slot & 1, place)
    return place


def owners_of(window, span_slot, group):
    return [
        span_slot[window[w, group * SPANS + span]] >> 1 for span in range(SPANS) for w in range(WIN)
    ]


def pack_slots(window, span_slot, cache_keys, cache_values, queries, out_weight, by_head, *refs):
    rest, lent = refs[:GROUPS], refs[GROUPS : GROUPS + 2]
    held, queries_held, lent_held, held_sems, sems = refs[GROUPS + 2 :]
    me = lax.axis_index("cache")
    rows, columns = lent[0].shape
    column = pl.multiple_of((1 - lax.axis_index("head")) * columns, HD)
    loads = [
        pltpu.make_async_copy(source, held.at[kv], held_sems.at[kv])
        for kv, source in enumerate((cache_keys, cache_values))
    ]
    source = queries.at[pl.ds(0, EARLY), :, pl.ds(0, WIDE)]
    loads.append(pltpu.make_async_copy(source, queries_held, held_sems.at[2]))
    for part in range(2):
        row = pl.multiple_of((2 * me + part) * rows, 16)
        source = out_weight.at[pl.ds(row, rows), pl.ds(column, columns)]
        loads.append(pltpu.make_async_copy(source, lent_held.at[part], held_sems.at[3 + part]))
    for load in loads:
        load.start()
    slots = [picked(window, span_slot, goes_to(me, step), me) for step in range(GROUPS)]
    for kv in range(2):
        loads[kv].wait()
        for head in range(SPACE):
            source = held.at[kv, :, :, pl.ds(head * HD, HD)]
            target = by_head.at[head, pl.ds(2 * kv, 2)]
            pltpu.make_async_copy(source, target, sems.at[0]).start()
    for step, slot in enumerate(slots):
        source = held.at[:, slot, :, pl.ds(WIDE, 2 * HD)]
        pltpu.make_async_copy(source, rest[step], sems.at[1 + step]).start()
    loads[2].wait()
    for head in range(SPACE):
        source = queries_held.at[:, :, pl.ds(head * HD, HD)]
        target = by_head.at[head, pl.ds(4, EARLY)]
        pltpu.make_async_copy(source, target, sems.at[0]).start()
    for part in range(2):
        loads[3 + part].wait()
        pltpu.make_async_copy(lent_held.at[part], lent[part], sems.at[1 + GROUPS + part]).start()
    for place, target in enumerate((by_head, *rest, *lent)):
        wait_for(target, sems.at[place])


def unit_of(kind, pair):
    return kind * PAIRS + pair - EARLY


def pack_pairs(queries, keys, values, sent, held, held_sems, sems):
    loads = [
        pltpu.make_async_copy(source, held.at[kind], held_sems.at[kind])
        for kind, source in enumerate((queries, keys, values))
    ]
    for load in loads:
        load.start()
    for kind in range(3):
        first = EARLY if kind == 0 else 0
        loads[kind].wait()
        for to in range(SPACE):
            wide, last = pl.ds(to * HD, HD), pl.ds(WIDE + to % 2 * HD, HD)
            if first < SPANS:
                pltpu.make_async_copy(
                    held.at[kind, pl.ds(first, SPANS - first), :, wide],
                    sent.at[to, pl.ds(unit_of(kind, first), SPANS - first)],
                    sems.at[kind],
                ).start()
            pltpu.make_async_copy(
                held.at[kind, to // 2, :, last], sent.at[to, unit_of(kind, SPANS)], sems.at[kind]
            ).start()
    for kind in range(3):
        first = EARLY if kind == 0 else 0
        wait_for(sent.at[:, pl.ds(unit_of(kind, first), PAIRS - first)], sems.at[kind])


def pack_cached(window, span_slot, by_head, *refs):
    rest, sent, wide = refs[:GROUPS], refs[GROUPS + 1], refs[GROUPS + 2 : 2 * GROUPS + 2]
    held, heads, held_sems, wide_sems, sent_sem = refs[2 * GROUPS + 2 :]
    group = lax.axis_index("cache")
    loads = [pltpu.make_async_copy(by_head.at[:, pl.ds(0, 4)], heads, held_sems.at[GROUPS])]
    for step in range(GROUPS):
        target = held.at[came_from(group, step)]
        loads.append(pltpu.make_async_copy(rest[step], target, held_sems.at[step]))
    for load in loads:
        load.start()
    slots = [picked(window, span_slot, goes_to(group, step), group) for step in range(GROUPS)]
    owners = owners_of(window, span_slot, group)
    loads[0].wait()
    for step, slot in enumerate(slots):
        for kv in range(2):
            source = heads.at[:, 2 * kv + slot]
            pltpu.make_async_copy(source, wide[step].at[kv], wide_sems.at[step]).start()
    for load in loads[1:]:
        load.wait()
    for to in range(SPACE):
        for w in range(WIN):
            owner = owners[to // 2 * WIN + w]
            pltpu.make_async_copy(
                held.at[owner, :, :, pl.ds(to % 2 * HD, HD)],
                sent.at[to, pl.ds(unit_of(3, 2 * w), 2)],
                sent_sem.at[0],
            ).start()
    for step in range(GROUPS):
        wait_for(wide[step], wide_sems.at[step])
    wait_for(sent.at[:, pl.ds(unit_of(3, 0), 2 * WIN)], sent_sem.at[0])


def attend(window, span_slot, counts, *refs):
    early, came, wide = refs[0], refs[1], refs[2 : 2 + GROUPS]
    out, q_all, k_all, v_all, sent, ready, left = refs[2 + GROUPS :]
    group = lax.axis_index("cache")
    me = lax.axis_index("space")
    factor = math.log2(math.e) / math.sqrt(HD)

    def fetch(pair, kind, source, target):
        pltpu.make_async_copy(source, target, ready.at[pair, kind]).start()

    def share(pair, kind, segment):
        if kind == 0:
            return q_all.at[pair]
        chunks = pl.ds(segment * SPACE, SPACE)
        if kind == 1:
            return k_all.at[pair, chunks]
        return v_all.at[pair, chunks, :, pl.ds(0, HD)]

    def fetch_pair(pair):
        for kind in range(3):
            before = kind == 0 and pair < EARLY
            source = early.at[:, 4 + pair] if before else came.at[:, unit_of(kind, pair)]
            fetch(pair, kind, source, share(pair, kind, 0))

    def fetch_wide(step, place):
        pair, segment = place >> 1, 1 + (place & 1)
        for kv in range(2):
            fetch(pair, 1 + kv, wide[step].at[kv], share(pair, 1 + kv, segment))

    fetch_pair(0)
    owners = owners_of(window, span_slot, group)
    places = []
    for step in range(GROUPS):
        source = came_from(group, step)
        place = jnp.int32(0)
        for entry, owner in enumerate(owners):
            place = jnp.where(owner == source, entry, place)
        places.append(place)
        pl.when(place < WIN)(lambda: fetch_wide(step, place))
    v_all[:, :, :, HD:] = jnp.ones((PAIRS, 3 * SPACE, ROWS, HD), jnp.bfloat16)

    def prepare(pair):
        for kind in range(3):
            wait_for(q_all.at[pair] if kind == 0 else k_all.at[pair], ready.at[pair, kind])
        span = me >> 1 if pair == SPANS else pair
        for w in range(WIN):
            limit = counts[window[w, group * SPANS + span]]
            first = (1 + w) * SPACE
            half = slice(first + SPACE // 2, first + SPACE)
            extent = (SPACE // 2, ROWS, HD)
            spots = SPAN // 2 + lax.broadcasted_iota(jnp.int32, extent, 1)
            valid = spots + ROWS * lax.broadcasted_iota(jnp.int32, extent, 0) < limit
            key = k_all[pair, first, 0:16].astype(jnp.float32)[0:1]
            key = jnp.broadcast_to(key[None], extent)
            held = k_all[pair, half].astype(jnp.float32)
            k_all[pair, half] = jnp.where(valid, held, key).astype(jnp.bfloat16)
            held = v_all[pair, half, :, 0:HD].astype(jnp.float32)
            v_all[pair, half, :, 0:HD] = jnp.where(valid, held, 0.0).astype(jnp.bfloat16)
            v_all[pair, half, :, HD:] = jnp.where(valid, 1.0, 0.0).astype(jnp.bfloat16)

    block = SPACE // BLOCKS

    def score(pair, part):
        query = q_all[pair, part * block : (part + 1) * block].reshape(block * ROWS, HD)
        key = k_all[pair].reshape(3 * SPAN, HD)
        return lax.dot_general(
            query, key, (((1,), (1,)), ((), ())), preferred_element_type=jnp.float32
        )

    def finish(pair, part, scores):
        top = jnp.max(scores, axis=1, keepdims=True)
        weights = jnp.exp2((scores - top) * factor).astype(jnp.bfloat16)
        value = v_all[pair].reshape(3 * SPAN, 2 * HD)
        both = jnp.dot(weights, value, preferred_element_type=jnp.float32)
        done = (both[:, 0:HD] / both[:, HD:]).astype(jnp.bfloat16).reshape(block, ROWS, HD)
        for place in range(block):
            for half in range(2):
                sent[2 * (part * block + place) + half, pair] = done[place]

    steps = [(pair, part) for pair in range(PAIRS) for part in range(BLOCKS)]
    prepare(0)
    for step, place in enumerate(places):
        pl.when(place >= WIN)(lambda: fetch_wide(step, place))
    for pair in range(1, PAIRS):
        fetch_pair(pair)
    for w in range(WIN):
        for kv in range(2):
            source = came.at[:, unit_of(3, 2 * w + kv)]
            fetch(SPANS, 1 + kv, source, share(SPANS, 1 + kv, 1 + w))
    scores = score(0, 0)
    for now, later in zip(steps, steps[1:] + [None]):
        held = scores
        if later is not None:
            if later[1] == 0:
                prepare(later[0])
            scores = score(*later)
        finish(*now, held)
        if now[1] == BLOCKS - 1:
            pair = now[0]
            pltpu.make_async_copy(sent.at[:, pair], out.at[:, pair], left.at[pair]).start()

    for pair in range(PAIRS):
        pltpu.make_async_copy(sent.at[:, pair], out.at[:, pair], left.at[pair]).wait()


def project(came, own_weight, *refs):
    lent, out, features, own, other, mixed, came_sems, weight_sems, out_sems = (
        refs[:GROUPS],
        *refs[GROUPS:],
    )
    group = lax.axis_index("cache")
    half = lax.axis_index("head")
    columns = out.shape[1]
    rows = lent[0].shape[0]
    tiles = weight_sems.shape[0]
    tile = columns // tiles
    for part in range(2):
        source = half if part == 0 else 1 - half
        for space in range(SPACE):
            pltpu.make_async_copy(
                came.at[2 * space + source, pl.ds(0, SPANS * ROWS)],
                features.at[part, :, pl.ds(space * HD, HD)],
                came_sems.at[part],
            ).start()
            pltpu.make_async_copy(
                came.at[2 * space + source, pl.ds(SPANS * ROWS, ROWS)],
                features.at[
                    part, pl.ds(space // 2 * ROWS, ROWS), pl.ds(WIDE + space % 2 * HD, HD)
                ],
                came_sems.at[part],
            ).start()

    def fetch(step):
        here = pl.ds(step * tile, tile)
        start = pl.multiple_of(half * columns + step * tile, 128)
        pltpu.make_async_copy(
            own_weight.at[:, pl.ds(start, tile)], own.at[step], weight_sems.at[step, 0]
        ).start()
        for place, chunk in enumerate(lent):
            holder = group ^ (place // 4)
            start = pl.multiple_of(came_from(holder, LENT[place % 4]) * rows, 16)
            pltpu.make_async_copy(
                chunk.at[:, here], other.at[step, pl.ds(start, rows)], weight_sems.at[step, 1]
            ).start()

    for step in range(AHEAD):
        fetch(step)
    for part in range(2):
        wait_for(features.at[part], came_sems.at[part])
    for step in range(tiles):
        here = pl.ds(step * tile, tile)
        wait_for(own.at[step], weight_sems.at[step, 0])
        wait_for(other.at[step], weight_sems.at[step, 1])
        if step + AHEAD < tiles:
            fetch(step + AHEAD)
        total = jnp.dot(features[0], own[step], preferred_element_type=jnp.float32)
        total += jnp.dot(features[1], other[step], preferred_element_type=jnp.float32)
        mixed[step] = total.astype(jnp.bfloat16)
        pltpu.make_async_copy(mixed.at[step], out.at[:, here], out_sems.at[step]).start()
    for step in range(tiles):
        here = pl.ds(step * tile, tile)
        pltpu.make_async_copy(mixed.at[step], out.at[:, here], out_sems.at[step]).wait()


def on_device(
    queries, keys, values, cache_keys, cache_values, window, span_slot, counts, out_weight
):
    bf16 = jnp.bfloat16
    shape = jax.ShapeDtypeStruct
    depth, width = out_weight.shape
    columns = width // 2

    rows = depth // GROUPS // 2
    window = window.T

    by_head, *sent = pl.pallas_call(
        pack_slots,
        out_shape=[shape((SPACE, 4 + EARLY, ROWS, HD), bf16)]
        + [shape((2, ROWS, 2 * HD), bf16)] * GROUPS
        + [shape((rows, columns), bf16)] * 2,
        in_specs=[SMEM] * 2 + [HBM] * 4,
        out_specs=[HBM] * (3 + GROUPS),
        scratch_shapes=[
            pltpu.VMEM((2, 2, ROWS, HEADS * HD), bf16),
            pltpu.VMEM((EARLY, ROWS, WIDE), bf16),
            pltpu.VMEM((2, rows, columns), bf16),
            pltpu.SemaphoreType.DMA((5,)),
            pltpu.SemaphoreType.DMA((3 + GROUPS,)),
        ],
        compiler_params=params(60),
        name="pack_slots",
    )(window, span_slot, cache_keys, cache_values, queries, out_weight)
    by_head, *sent, queries = lax.optimization_barrier((by_head, *sent, queries))
    rest, lent = sent[:GROUPS], sent[GROUPS:]
    by_head = lax.all_to_all(
        by_head.reshape(SPACE, -1, HD), "space", split_axis=0, concat_axis=0, tiled=True
    ).reshape(by_head.shape)
    rest = [rest[0]] + [shift(rest[step], "cache", step) for step in range(1, GROUPS)]
    lent = [
        lax.ppermute(lent[0], "head", [(0, 1), (1, 0)]),
        lax.ppermute(lent[1], ("space", "head"), [(i, i ^ 3) for i in range(2 * SPACE)]),
    ]
    pairs = pl.pallas_call(
        pack_pairs,
        out_shape=shape((SPACE, UNITS, ROWS, HD), bf16),
        in_specs=[HBM] * 3,
        out_specs=HBM,
        scratch_shapes=[
            pltpu.VMEM((3, SPANS, ROWS, HEADS * HD), bf16),
            pltpu.SemaphoreType.DMA((3,)),
            pltpu.SemaphoreType.DMA((3,)),
        ],
        compiler_params=params(60),
        name="pack_pairs",
    )(queries, keys, values)
    by_head, *rest = lax.optimization_barrier((by_head, *rest))
    pairs, *wide = pl.pallas_call(
        pack_cached,
        out_shape=[shape(pairs.shape, bf16)] + [shape((2, SPACE, ROWS, HD), bf16)] * GROUPS,
        in_specs=[SMEM] * 2 + [HBM] * (2 + GROUPS),
        out_specs=[HBM] * (1 + GROUPS),
        input_output_aliases={3 + GROUPS: 0},
        scratch_shapes=[
            pltpu.VMEM((GROUPS, 2, ROWS, 2 * HD), bf16),
            pltpu.VMEM((SPACE, 4, ROWS, HD), bf16),
            pltpu.SemaphoreType.DMA((GROUPS + 1,)),
            pltpu.SemaphoreType.DMA((GROUPS,)),
            pltpu.SemaphoreType.DMA((1,)),
        ],
        compiler_params=params(60),
        name="pack_cached",
    )(window, span_slot, by_head, *rest, pairs)
    pairs, *lent = lax.optimization_barrier((pairs, *lent))
    came = lax.all_to_all(
        pairs.reshape(SPACE, UNITS * ROWS, HD), "space", split_axis=0, concat_axis=0, tiled=True
    ).reshape(pairs.shape)
    wide = [wide[0]] + [shift(wide[step], "cache", step) for step in range(1, GROUPS)]
    lent = jnp.concatenate(lent, 0)
    lent, *wide = lax.optimization_barrier((lent, *wide))
    lent = [lent] + [shift(lent, "cache", step) for step in LENT[1:]]
    lent += [lax.ppermute(chunk, "cache", [(i, i ^ 1) for i in range(8)]) for chunk in lent]

    attended = pl.pallas_call(
        attend,
        out_shape=shape((2 * SPACE, PAIRS, ROWS, HD), bf16),
        in_specs=[SMEM] * 3 + [HBM] * (2 + GROUPS),
        out_specs=HBM,
        scratch_shapes=[
            pltpu.VMEM((PAIRS, SPACE, ROWS, HD), bf16),
            pltpu.VMEM((PAIRS, 3 * SPACE, ROWS, HD), bf16),
            pltpu.VMEM((PAIRS, 3 * SPACE, ROWS, 2 * HD), bf16),
            pltpu.VMEM((2 * SPACE, PAIRS, ROWS, HD), bf16),
            pltpu.SemaphoreType.DMA((PAIRS, 3)),
            pltpu.SemaphoreType.DMA((PAIRS,)),
        ],
        compiler_params=params(60),
        name="attend",
    )(window, span_slot, counts, by_head, came, *wide)
    attended = attended.reshape(2 * SPACE, PAIRS * ROWS, HD)
    attended = lax.all_to_all(
        attended, ("space", "head"), split_axis=0, concat_axis=0, tiled=True
    )

    tile = 512
    tiles = columns // tile
    mixed = pl.pallas_call(
        project,
        out_shape=shape((SPANS * ROWS, columns), bf16),
        in_specs=[HBM] * (2 + GROUPS),
        out_specs=HBM,
        scratch_shapes=[
            pltpu.VMEM((2, SPANS * ROWS, depth), bf16),
            pltpu.VMEM((tiles, depth, tile), bf16),
            pltpu.VMEM((tiles, depth, tile), bf16),
            pltpu.VMEM((tiles, SPANS * ROWS, tile), bf16),
            pltpu.SemaphoreType.DMA((2,)),
            pltpu.SemaphoreType.DMA((tiles, 2)),
            pltpu.SemaphoreType.DMA((tiles,)),
        ],
        compiler_params=params(52),
        name="project",
    )(attended, out_weight, *lent)
    return mixed.reshape(SPANS, ROWS, columns)


def solution(mesh):
    in_specs = (
        P("cache", "space", "head"),
        P("cache", "space", "head"),
        P("cache", "space", "head"),
        P("cache", "space", "head"),
        P("cache", "space", "head"),
        P(),
        P(),
        P(),
        P("head", None),
    )
    out_specs = P("cache", "space", "head")
    return jax.shard_map(
        on_device, mesh=mesh, in_specs=in_specs, out_specs=out_specs, check_vma=False
    )
```
